32 devices in a mesh: dp: 4 (over y, x), vocab: 8 (over z, core).
Axes of the slice: x: 2, y: 2, z: 4, core: 2. Of those that a mesh axis runs over, the one named last changes fastest.
Arguments:
- hidden: bfloat16 [512, 3072], P('dp')
- head: bfloat16 [4, 8192, 3072], P('dp', 'vocab')
- teacher: bfloat16 [512, 32768], P('dp', 'vocab')
- shard_order: int32 [8], replicated, may hold values from 0 to 7, each once
- loss_weight: float32 [512], replicated, may hold values from 256 to 2048
Outputs:
- head_grad: bfloat16 [4, 8192, 3072], P('dp', 'vocab')
- divergence: float32 [512], replicated
The draws below stay inside these ranges and needn't reach their ends.
Inputs may be any that keep to these rules, and one draw needn't show every extreme that they name: `shard_order`: each block number appears once.
All inputs are finite; a program needn't handle non-finite values.
Results may differ from the reference program's by a relative error of at most 0.0048.
Values may be sent and summed in bfloat16 or wider, within the bound.
No kernel may reach another device: no remote copies, remote signals or barrier semaphores. Data moves between devices by JAX's collectives and lax.ppermute only.
A program may use at most 128 MiB of HBM per device.

```python
import math
import jax
import jax.numpy as jnp
from jax import lax

D = 3072
VOC_DEV = 4096
TOKENS = 512
V = 32768
SUB = 1024
HEAD_ROWS = 8192
N_DP = 4
N_VOCAB = 8


def head_base(key):
    return jax.random.normal(key, (N_DP, V // N_DP, D), jnp.float32)


def draw_head(key, part):
    base_rows = head_base(key)
    return (base_rows * (1.0 / jnp.sqrt(jnp.float32(D)))).astype(jnp.bfloat16)


def draw_hidden(key, part):
    key = jax.random.fold_in(key, 2)
    return jnp.clip(jax.random.normal(key, (TOKENS, D), jnp.float32), -6.0, 6.0).astype(jnp.bfloat16)


def draw_teacher(key, part):
    key = jax.random.fold_in(key, 3)
    keys = jax.random.split(key, 1)
    values = jax.random.normal(keys[0], (TOKENS, V), jnp.float32)
    return jnp.clip(values, -6.0, 6.0).astype(jnp.bfloat16)


def setup_inputs(seed: int = 0) -> dict:
    arg_keys = jax.random.split(jax.random.key(seed), 6)
    return {
        "hidden": draw_hidden(jax.random.fold_in(arg_keys[5], 71), 0),
        "head": draw_head(jax.random.fold_in(arg_keys[5], 71), 0),
        "teacher": draw_teacher(jax.random.fold_in(arg_keys[5], 71), 0),
        "shard_order": jax.random.permutation(arg_keys[3], N_VOCAB).astype(jnp.int32),
        "loss_weight": jnp.clip(jnp.exp(jax.random.uniform(arg_keys[4], (TOKENS,), jnp.float32, math.log(256.0), math.log(2048.0))), 256.0, 2048.0),
    }


def reference(hidden, head, teacher, shard_order, loss_weight):
    table = head.reshape(N_DP, N_VOCAB, SUB, D).transpose(1, 0, 2, 3).reshape(N_VOCAB, VOC_DEV, D)
    ordinal = jnp.arange(N_VOCAB, dtype=jnp.int32)
    matches = (shard_order[None, :] == ordinal[:, None]).astype(jnp.int32)
    inverse = lax.optimization_barrier(jnp.sum(matches * ordinal[None, :], axis=1)).astype(jnp.int32)
    blocks = teacher.reshape(TOKENS, N_VOCAB, VOC_DEV)

    def block_target(block_id):
        return lax.dynamic_index_in_dim(blocks, inverse[block_id], 1, keepdims=False).astype(jnp.float32)

    def gather_stats(running, block_id):
        top_s, sum_s, top_t, sum_t, cross = running
        rows = lax.dynamic_index_in_dim(table, block_id, 0, keepdims=False)
        scores = lax.dot_general(hidden, rows, (((1,), (1,)), ((), ())), preferred_element_type=jnp.float32)
        target = block_target(block_id)
        next_s = jnp.maximum(top_s, lax.optimization_barrier(jnp.max(scores, axis=1)))
        next_t = jnp.maximum(top_t, lax.optimization_barrier(jnp.max(target, axis=1)))
        sum_s = sum_s * jnp.exp(top_s - next_s) + lax.optimization_barrier(jnp.sum(jnp.exp(scores - next_s[:, None]), axis=1))
        exp_t = jnp.exp(target - next_t[:, None])
        factor = jnp.exp(top_t - next_t)
        sum_t = sum_t * factor + lax.optimization_barrier(jnp.sum(exp_t, axis=1))
        cross = cross * factor + lax.optimization_barrier(jnp.sum(exp_t * (target - scores), axis=1))
        return ((next_s, sum_s, next_t, sum_t, cross), scores)
    lowest = jnp.full((TOKENS,), -jnp.inf, jnp.float32)
    nothing = jnp.zeros((TOKENS,), jnp.float32)
    start = (lowest, nothing, lowest, nothing, nothing)
    (top_s, sum_s, top_t, sum_t, cross), scores = lax.scan(gather_stats, start, ordinal)
    divergence = cross / sum_t - top_t - jnp.log(sum_t) + top_s + jnp.log(sum_s)

    def block_grad(inputs):
        block_scores, block_id = inputs
        target = block_target(block_id)
        prob_s = jnp.exp(block_scores - top_s[:, None]) / sum_s[:, None]
        prob_t = jnp.exp(target - top_t[:, None]) / sum_t[:, None]
        logit_grad = (loss_weight[:, None] * (prob_s - prob_t)).astype(jnp.bfloat16)
        result = lax.dot_general(logit_grad, hidden, (((0,), (0,)), ((), ())), preferred_element_type=jnp.float32)
        return result.astype(jnp.bfloat16)
    grads = lax.map(block_grad, (scores, ordinal))
    head_grad = grads.reshape(N_VOCAB, N_DP, SUB, D).transpose(1, 0, 2, 3).reshape(N_DP, HEAD_ROWS, D)
    return (head_grad, divergence)
```

```python
import functools
import itertools

import jax
import jax.numpy as jnp
import numpy as np
from jax import lax
from jax.experimental import pallas as pl
from jax.experimental.pallas import tpu as pltpu
from jax.sharding import PartitionSpec as P

MIB = 1024 * 1024
LOWEST = float(np.finfo(np.float32).min)
NO_PLAN = 2**30


def xor_permute(x, axis, k):
    size = lax.axis_size(axis)
    return lax.ppermute(x, axis, [(i, i ^ k) for i in range(size)])


def gather_all(x):
    count = lax.axis_size("dp") * lax.axis_size("vocab")
    copies = jnp.broadcast_to(x[None], (count, *x.shape))
    return lax.all_to_all(copies, ("dp", "vocab"), split_axis=0, concat_axis=0, tiled=True)


def log_sum_exp(parts, axis):
    top = jnp.max(parts, axis=axis, keepdims=True)
    total = jnp.sum(jnp.exp(parts - top), axis=axis, keepdims=True)
    return jnp.squeeze(top + jnp.log(total), axis)


def combine_stats(parts, tokens):
    n_dp, n_vocab = lax.axis_size("dp"), lax.axis_size("vocab")
    student = log_sum_exp(parts[:, 0, :tokens], 0)
    target = log_sum_exp(parts[:, 0, tokens:].reshape(n_dp, n_vocab, tokens // n_dp), 1)
    return student, target.reshape(tokens)


def place(rows):
    return lambda k: pl.multiple_of((lax.axis_index("dp") ^ k) * rows, rows)


def student_kernel(n_dp, n_chunks, *refs):
    chunk_refs = refs[:n_chunks]
    head_ref, teacher_ref, out_ref, hid_out_ref, stats_ref, hid_ref, top_ref, sum_ref, stat_ref = refs[
        n_chunks:-2
    ]
    sems, out_sem = refs[-2:]
    step, last = pl.program_id(0), pl.num_programs(0) - 1
    tokens = hid_ref.shape[0]
    rows = teacher_ref.shape[0]
    half = rows // 2

    @pl.when(step == 0)
    def _():
        core = lax.axis_index("vocab") & 1
        starts = [k * rows for k in range(n_dp)]
        if n_chunks > n_dp:
            starts[-1] += core * half
            starts.append((n_dp - 1) * rows + (1 - core) * half)
        copies = []
        for i, (ref, start) in enumerate(zip(chunk_refs, starts)):
            target = hid_ref.at[pl.ds(pl.multiple_of(start, half), ref.shape[0])]
            copies.append(pltpu.make_async_copy(ref, target, sems.at[i]))
        for copy in copies:
            copy.start()
        top_ref[...] = jnp.full(top_ref.shape, LOWEST, jnp.float32)
        sum_ref[...] = jnp.zeros(sum_ref.shape, jnp.float32)
        values = teacher_ref[...].astype(jnp.float32)
        top = jnp.max(values, axis=1, keepdims=True)
        total = jnp.sum(jnp.exp(values - top), axis=1, keepdims=True)
        stat = jnp.broadcast_to(top + jnp.log(total), (rows, 128))
        stats_ref[:, tokens:] = jnp.transpose(stat)[0:1]
        for copy in copies:
            copy.wait()

    hid_copy = pltpu.make_async_copy(hid_ref, hid_out_ref, out_sem)

    @pl.when(step == 0)
    def _():
        hid_copy.start()

    part = min(256, tokens)
    for first in range(0, tokens, part):
        here = slice(first, first + part)
        scores = lax.dot_general(
            hid_ref[here], head_ref[0], (((1,), (1,)), ((), ())), preferred_element_type=jnp.float32
        )
        out_ref[here] = scores
        old = top_ref[here]
        top = jnp.maximum(old, jnp.max(scores, axis=1, keepdims=True))
        total = jnp.sum(jnp.exp(scores - top), axis=1, keepdims=True)
        top_ref[here] = top
        sum_ref[here] = sum_ref[here] * jnp.exp(old - top) + total

    @pl.when(step == last)
    def _():
        at = place(rows)
        stat = top_ref[...] + jnp.log(sum_ref[...])
        for k in range(n_dp):
            here = stat[k * rows : (k + 1) * rows]
            stat_ref[pl.ds(at(k), rows)] = jnp.broadcast_to(here, (rows, 128))
        stats_ref[:, :tokens] = jnp.transpose(stat_ref[...])[0:1]
        hid_copy.wait()


def student_call(chunks, head, teacher, tokens):
    n_dp = lax.axis_size("dp")
    _, rows, depth = head.shape
    block = min(256, rows)
    return pl.pallas_call(
        functools.partial(student_kernel, n_dp, len(chunks)),
        grid=(rows // block,),
        in_specs=[pl.BlockSpec(memory_space=pl.ANY)] * len(chunks)
        + [
            pl.BlockSpec((1, block, depth), lambda i: (0, i, 0)),
            pl.BlockSpec(teacher.shape, lambda i: (0, 0)),
        ],
        out_specs=[
            pl.BlockSpec((tokens, block), lambda i: (0, i)),
            pl.BlockSpec(memory_space=pl.ANY),
            pl.BlockSpec((1, tokens + teacher.shape[0]), lambda i: (0, 0)),
        ],
        out_shape=[
            jax.ShapeDtypeStruct((tokens, rows), jnp.float32),
            jax.ShapeDtypeStruct((tokens, depth), jnp.bfloat16),
            jax.ShapeDtypeStruct((1, tokens + teacher.shape[0]), jnp.float32),
        ],
        scratch_shapes=[
            pltpu.VMEM((tokens, depth), jnp.bfloat16),
            pltpu.VMEM((tokens, 1), jnp.float32),
            pltpu.VMEM((tokens, 1), jnp.float32),
            pltpu.VMEM((tokens, 128), jnp.float32),
            pltpu.SemaphoreType.DMA((len(chunks),)),
            pltpu.SemaphoreType.DMA,
        ],
        compiler_params=pltpu.CompilerParams(vmem_limit_bytes=48 * MIB),
        cost_estimate=pl.CostEstimate(
            flops=2 * tokens * rows * depth,
            bytes_accessed=2 * rows * depth + 2 * tokens * depth + 4 * tokens * rows,
            transcendentals=tokens * rows,
        ),
        name="student",
    )(*chunks, head, teacher)


def logit_grad_kernel(
    flags_ref, mine_ref, got_ref, scores_ref, scales_ref, grad_ref, cross_ref, col_ref
):
    step, last = pl.program_id(0), pl.num_programs(0) - 1
    rows = scores_ref.shape[0]
    half = rows // 2
    at = place(rows)(step)

    @pl.when(step == 0)
    def _():
        col_ref[...] = jnp.transpose(jnp.concatenate([scales_ref[...]] * 16))

    keep = flags_ref[1] != 0
    for first in (0, half):
        part = slice(first, first + half)
        here = pl.ds(pl.multiple_of(at + first, half), half)
        scales = col_ref[here]
        student = scores_ref[part]
        target = jnp.where(keep, mine_ref[0, part], got_ref[0, part]).astype(jnp.float32)
        prob_s = jnp.exp(student - scales[:, 0:1])
        prob_t = jnp.exp(target - scales[:, 1:2])
        cross = jnp.sum(prob_t * (target - student), axis=1, keepdims=True)
        grad = scales[:, 2:3] * (prob_s - prob_t)
        grad_ref[part] = grad.astype(jnp.bfloat16)
        col_ref[here] = jnp.broadcast_to(cross, (half, 128))

    @pl.when(step == last)
    def _():
        cross_ref[...] = jnp.transpose(col_ref[...])[0:1]


def logit_grad_call(flags, mine, got, scores, scales):
    n_dp, part, rows = mine.shape
    tokens = n_dp * part
    return pl.pallas_call(
        logit_grad_kernel,
        grid=(n_dp,),
        in_specs=[
            pl.BlockSpec(memory_space=pltpu.SMEM),
            pl.BlockSpec((1, part, rows), lambda k: (k, 0, 0)),
            pl.BlockSpec((1, part, rows), lambda k: (k, 0, 0)),
            pl.BlockSpec((part, rows), lambda k: (k, 0)),
            pl.BlockSpec((8, tokens), lambda k: (0, 0)),
        ],
        out_specs=[
            pl.BlockSpec((part, rows), lambda k: (k, 0)),
            pl.BlockSpec((1, tokens), lambda k: (0, 0)),
        ],
        out_shape=[
            jax.ShapeDtypeStruct((tokens, rows), jnp.bfloat16),
            jax.ShapeDtypeStruct((1, tokens), jnp.float32),
        ],
        scratch_shapes=[pltpu.VMEM((tokens, 128), jnp.float32)],
        compiler_params=pltpu.CompilerParams(vmem_limit_bytes=24 * MIB),
        cost_estimate=pl.CostEstimate(
            flops=8 * tokens * rows, bytes_accessed=8 * tokens * rows, transcendentals=2 * tokens * rows
        ),
        name="logit_grad",
    )(flags, mine, got, scores, scales)


def head_grad_kernel(grad_ref, hid_ref, out_ref):
    out_ref[0] = lax.dot_general(
        grad_ref[...], hid_ref[...], (((0,), (0,)), ((), ())), preferred_element_type=jnp.float32
    ).astype(jnp.bfloat16)


def head_grad_call(logit_grad, hid):
    tokens, rows = logit_grad.shape
    depth = hid.shape[1]
    block = min(256, rows)
    return pl.pallas_call(
        head_grad_kernel,
        grid=(rows // block,),
        in_specs=[
            pl.BlockSpec((tokens, block), lambda i: (0, i)),
            pl.BlockSpec((tokens, depth), lambda i: (0, 0)),
        ],
        out_specs=pl.BlockSpec((1, block, depth), lambda i: (0, i, 0)),
        out_shape=jax.ShapeDtypeStruct((1, rows, depth), jnp.bfloat16),
        compiler_params=pltpu.CompilerParams(vmem_limit_bytes=48 * MIB),
        cost_estimate=pl.CostEstimate(
            flops=2 * tokens * rows * depth,
            bytes_accessed=2 * rows * depth + 2 * tokens * depth,
            transcendentals=0,
        ),
        name="head_grad",
    )(logit_grad, hid)


def chip_plans(n):
    def load(pair):
        ups = [sum(z < c <= p[z] for p in pair for z in range(n)) for c in range(1, n)]
        return max(ups), sum(ups)

    best = {}
    perms = list(itertools.permutations(range(n)))
    for pair in itertools.combinations_with_replacement(perms, 2):
        code = sum(3 ** (n * z + p[z]) for p in pair for z in range(n))
        if code not in best or load(pair) < load(best[code]):
            best[code] = pair
    return sorted(best.items())


def plan_tables(plans, n):
    codes = [code for code, _ in plans]
    keys = [
        (i << 8) | sum(first[z] << (2 * z) for z in range(n)) for i, (_, (first, _)) in enumerate(plans)
    ]
    pad = -len(codes) % 1024
    codes = np.array(codes + [-1] * pad, np.int32).reshape(-1, 128)
    keys = np.array(keys + [NO_PLAN] * pad, np.int32).reshape(-1, 128)
    return codes, keys


def plan_kernel(n_chips, order_ref, codes_ref, keys_ref, number_ref, flags_ref):
    chip = lax.axis_index("vocab") // 2
    code = jnp.int32(0)
    for block in range(2 * n_chips):
        dest = order_ref[block] // 2
        power = jnp.int32(0)
        for d in range(n_chips):
            power = jnp.where(dest == d, 3 ** (n_chips * (block // 2) + d), power)
        code = code + power
    key = jnp.min(jnp.where(codes_ref[...] == code, keys_ref[...], NO_PLAN))
    sends = jnp.int32(0)
    arrives = jnp.int32(0)
    for z in range(n_chips):
        goes = (key >> (2 * z)) & 3
        source = jnp.where(order_ref[2 * z] // 2 == goes, 0, 1)
        meant = jnp.where(source == 0, order_ref[2 * z], order_ref[2 * z + 1]) & 1
        sends = jnp.where(chip == z, source, sends)
        arrives = jnp.where(goes == chip, meant, arrives)
    number_ref[0] = key >> 8
    flags_ref[0] = 1 - sends
    flags_ref[1] = 1 - arrives


def plan_chips(shard_order, plans, n_chips):
    codes, keys = plan_tables(plans, n_chips)
    in_smem = pl.BlockSpec(memory_space=pltpu.SMEM)
    in_vmem = pl.BlockSpec(memory_space=pltpu.VMEM)
    return pl.pallas_call(
        functools.partial(plan_kernel, n_chips),
        in_specs=[in_smem, in_vmem, in_vmem],
        out_specs=[in_smem] * 2,
        out_shape=[jax.ShapeDtypeStruct((n,), jnp.int32) for n in (1, 2)],
        compiler_params=pltpu.CompilerParams(vmem_limit_bytes=60 * MIB),
        name="plan",
    )(shard_order, jnp.asarray(codes), jnp.asarray(keys))


def pick_kernel(flags_ref, mine_ref, other_ref, out_ref):
    dp = lax.axis_index("dp")
    n_dp, _, cols = out_ref.shape
    own = flags_ref[0] != 0
    for k in range(n_dp):
        here = pl.ds(pl.multiple_of((dp ^ k) * cols, cols), cols)
        out_ref[k] = jnp.where(own, mine_ref[:, here], other_ref[:, here])


def pick_call(flags, mine, other):
    n_dp = lax.axis_size("dp")
    shape = (n_dp, mine.shape[0], mine.shape[1] // n_dp)
    in_vmem = pl.BlockSpec(memory_space=pltpu.VMEM)
    return pl.pallas_call(
        pick_kernel,
        in_specs=[pl.BlockSpec(memory_space=pltpu.SMEM), in_vmem, in_vmem],
        out_specs=in_vmem,
        out_shape=jax.ShapeDtypeStruct(shape, jnp.bfloat16),
        compiler_params=pltpu.CompilerParams(vmem_limit_bytes=24 * MIB),
        name="pick",
    )(flags, mine, other)


def join_kernel(*refs):
    for k, ref in enumerate(refs[:-1]):
        refs[-1][k] = ref[...]


def join_call(pieces):
    in_vmem = pl.BlockSpec(memory_space=pltpu.VMEM)
    return pl.pallas_call(
        join_kernel,
        in_specs=[in_vmem] * len(pieces),
        out_specs=in_vmem,
        out_shape=jax.ShapeDtypeStruct((len(pieces), *pieces[0].shape), jnp.bfloat16),
        compiler_params=pltpu.CompilerParams(vmem_limit_bytes=24 * MIB),
        name="join",
    )(*pieces)


def halves(x):
    half = x.shape[0] // 2
    core = lax.axis_index("vocab") & 1
    mine = lax.dynamic_slice_in_dim(x, core * half, half, 0)
    return mine, lax.dynamic_slice_in_dim(x, (1 - core) * half, half, 0)


def over_dp(pieces):
    return [pieces[0]] + [xor_permute(pieces[k], "dp", k) for k in range(1, len(pieces))]


def wide_block(teacher, shard_order):
    token_rows = teacher.shape[0]
    n_vocab = lax.axis_size("vocab")
    piece_cols = teacher.shape[1] // n_vocab
    split_view = teacher.reshape(token_rows, n_vocab, piece_cols)
    spread_view = lax.all_to_all(split_view, "vocab", split_axis=1, concat_axis=1, tiled=True)
    ordinal = jnp.arange(n_vocab, dtype=jnp.int32)
    matches = (shard_order[None, :] == ordinal[:, None]).astype(jnp.int32)
    inverse = jnp.sum(matches * ordinal[None, :], axis=1)
    sorted_view = jnp.take(spread_view, inverse, axis=1)
    return lax.all_to_all(sorted_view, "vocab", split_axis=1, concat_axis=1, tiled=True).reshape(
        token_rows, n_vocab * piece_cols
    )


def on_device(hidden, head, teacher, shard_order, loss_weight):
    n_dp, n_vocab = lax.axis_size("dp"), lax.axis_size("vocab")
    n_chips = n_vocab // 2
    tokens = hidden.shape[0] * n_dp

    if n_chips <= 4:
        other = xor_permute(teacher, "vocab", 1)
        plans = chip_plans(n_chips)
        number, flags = plan_chips(shard_order, plans, n_chips)
        chunks = [hidden] + [xor_permute(hidden, "dp", k) for k in range(1, n_dp - 1)]
        hidden_mine, _ = halves(hidden)
        far = xor_permute(hidden_mine, "dp", n_dp - 1)

        def over_chips(x, pair):
            pairs = [(2 * z + c, 2 * pair[c][z] + c) for z in range(n_chips) for c in range(2)]
            return lax.ppermute(x, "vocab", pairs)

        arrived = lax.switch(
            number[0],
            [functools.partial(over_chips, pair=pair) for _, pair in plans],
            pick_call(flags, teacher, other),
        )
        chunks, far, arrived = lax.optimization_barrier((chunks, far, arrived))
        chunks += [far, xor_permute(far, "vocab", 1)]
        pieces = over_dp([arrived[k] for k in range(n_dp)])
        student, hid, stats = student_call(chunks, head, teacher, tokens)
        pieces, stats = lax.optimization_barrier((pieces, stats))
        mine = join_call(pieces)
        got = xor_permute(mine, "vocab", 1)
    else:
        chunks = [hidden] + [xor_permute(hidden, "dp", k) for k in range(1, n_dp)]
        student, hid, stats = student_call(chunks, head, teacher, tokens)
        block = wide_block(teacher, shard_order)
        cols, dp = block.shape[1] // n_dp, lax.axis_index("dp")
        mine = jnp.stack(
            over_dp([lax.dynamic_slice_in_dim(block, (dp ^ k) * cols, cols, 1) for k in range(n_dp)])
        )
        flags, got = jnp.ones((2,), jnp.int32), mine

    total_s, total_t = combine_stats(gather_all(stats), tokens)
    scales = jnp.stack([total_s, total_t, loss_weight, loss_weight] * 2)
    logit_grad, cross = logit_grad_call(flags, mine, got, student, scales)
    head_grad = head_grad_call(logit_grad, hid)
    divergence = jnp.sum(gather_all(cross), axis=(0, 1)) - total_t + total_s
    return head_grad, divergence


def solution(mesh):
    in_specs = (P("dp", None), P("dp", "vocab", None), P("dp", "vocab"), P(), P())
    out_specs = (P("dp", "vocab", None), P())
    return jax.shard_map(
        on_device, mesh=mesh, in_specs=in_specs, out_specs=out_specs, check_vma=False
    )
```

```python
import functools
import itertools

import jax
import jax.numpy as jnp
import numpy as np
from jax import lax
from jax.experimental import pallas as pl
from jax.experimental.pallas import tpu as pltpu
from jax.sharding import PartitionSpec as P

MIB = 1024 * 1024
LOWEST = float(np.finfo(np.float32).min)
NO_PLAN = 2**30


def xor_permute(x, axis, k):
    size = lax.axis_size(axis)
    return lax.ppermute(x, axis, [(i, i ^ k) for i in range(size)])


def device_count():
    return lax.axis_size("dp") * lax.axis_size("vocab")


def exchange(copies):
    return lax.all_to_all(copies, ("dp", "vocab"), split_axis=0, concat_axis=0, tiled=True)


def log_sum_exp(parts, axis):
    top = jnp.max(parts, axis=axis, keepdims=True)
    total = jnp.sum(jnp.exp(parts - top), axis=axis, keepdims=True)
    return jnp.squeeze(top + jnp.log(total), axis)


def combine_stats(parts, tokens):
    n_dp, n_vocab = lax.axis_size("dp"), lax.axis_size("vocab")
    student = log_sum_exp(parts[:, 0, :tokens], 0)
    target = log_sum_exp(parts[:, 0, tokens:].reshape(n_dp, n_vocab, tokens // n_dp), 1)
    return student, target.reshape(tokens)


def place(rows):
    return lambda k: pl.multiple_of((lax.axis_index("dp") ^ k) * rows, rows)


def student_kernel(n_chunks, *refs):
    chunk_refs = refs[:n_chunks]
    head_ref, teacher_ref, out_ref, hid_out_ref, stats_ref = refs[n_chunks : n_chunks + 5]
    hid_ref, rows_ref, logits_ref, scores_ref, top_ref, sum_ref, stat_ref = refs[n_chunks + 5 : -4]
    chunk_sems, head_sems, out_sems, sems = refs[-4:]
    tokens, rows = scores_ref.shape
    own = teacher_ref.shape[0]
    block = min(256, rows)
    blocks = rows // block

    def head_copy(i):
        here = pl.ds(pl.multiple_of(i * block, block), block)
        return pltpu.make_async_copy(head_ref.at[0, here], rows_ref.at[here], head_sems.at[i])

    def out_copy(i):
        here = pl.ds(pl.multiple_of(i * block, block), block)
        return pltpu.make_async_copy(scores_ref.at[:, here], out_ref.at[:, here], out_sems.at[i])

    teacher_copy = pltpu.make_async_copy(teacher_ref, logits_ref, sems.at[0])
    hid_copy = pltpu.make_async_copy(hid_ref, hid_out_ref, sems.at[1])
    copies = []
    for k, ref in enumerate(chunk_refs):
        copies.append(
            pltpu.make_async_copy(ref, hid_ref.at[k * own : (k + 1) * own], chunk_sems.at[k])
        )
    teacher_copy.start()
    for copy in copies:
        copy.start()
    for i in range(blocks):
        head_copy(i).start()

    top_ref[...] = jnp.full(top_ref.shape, LOWEST, jnp.float32)
    sum_ref[...] = jnp.zeros(sum_ref.shape, jnp.float32)
    teacher_copy.wait()
    values = logits_ref[...].astype(jnp.float32)
    top = jnp.max(values, axis=1, keepdims=True)
    total = jnp.sum(jnp.exp(values - top), axis=1, keepdims=True)
    stat = jnp.transpose(jnp.broadcast_to(top + jnp.log(total), (own, 128)))[0:1]
    stats_ref[:, :, tokens:] = jnp.broadcast_to(stat[None], (stats_ref.shape[0], 1, own))
    for copy in copies:
        copy.wait()
    hid_copy.start()

    def step(i, carry):
        columns = pl.ds(pl.multiple_of(i * block, block), block)
        head_copy(i).wait()
        part = min(256, tokens)
        for first in range(0, tokens, part):
            here = slice(first, first + part)
            scores = lax.dot_general(
                hid_ref[here],
                rows_ref[columns],
                (((1,), (1,)), ((), ())),
                preferred_element_type=jnp.float32,
            )
            scores_ref[here, columns] = scores
            old = top_ref[here]
            top = jnp.maximum(old, jnp.max(scores, axis=1, keepdims=True))
            total = jnp.sum(jnp.exp(scores - top), axis=1, keepdims=True)
            top_ref[here] = top
            sum_ref[here] = sum_ref[here] * jnp.exp(old - top) + total
        out_copy(i).start()
        return carry

    lax.fori_loop(0, blocks, step, 0)
    at = place(own)
    for k in range(n_chunks):
        here = slice(k * own, (k + 1) * own)
        stat = top_ref[here] + jnp.log(sum_ref[here])
        stat_ref[pl.ds(at(k), own)] = jnp.broadcast_to(stat, (own, 128))
    stat = jnp.transpose(stat_ref[...])[0:1]
    stats_ref[:, :, :tokens] = jnp.broadcast_to(stat[None], (stats_ref.shape[0], 1, tokens))
    for i in range(blocks):
        out_copy(i).wait()
    hid_copy.wait()


def student_call(chunks, head, teacher, tokens):
    _, rows, depth = head.shape
    blocks = rows // min(256, rows)
    in_hbm = pl.BlockSpec(memory_space=pltpu.HBM)
    return pl.pallas_call(
        functools.partial(student_kernel, len(chunks)),
        in_specs=[in_hbm] * (len(chunks) + 2),
        out_specs=[in_hbm, in_hbm, pl.BlockSpec(memory_space=pltpu.VMEM)],
        out_shape=[
            jax.ShapeDtypeStruct((tokens, rows), jnp.float32),
            jax.ShapeDtypeStruct((tokens, depth), jnp.bfloat16),
            jax.ShapeDtypeStruct((device_count(), 1, tokens + teacher.shape[0]), jnp.float32),
        ],
        scratch_shapes=[
            pltpu.VMEM((tokens, depth), jnp.bfloat16),
            pltpu.VMEM((rows, depth), jnp.bfloat16),
            pltpu.VMEM(teacher.shape, jnp.bfloat16),
            pltpu.VMEM((tokens, rows), jnp.float32),
            pltpu.VMEM((tokens, 1), jnp.float32),
            pltpu.VMEM((tokens, 1), jnp.float32),
            pltpu.VMEM((tokens, 128), jnp.float32),
            pltpu.SemaphoreType.DMA((len(chunks),)),
            pltpu.SemaphoreType.DMA((blocks,)),
            pltpu.SemaphoreType.DMA((blocks,)),
            pltpu.SemaphoreType.DMA((2,)),
        ],
        compiler_params=pltpu.CompilerParams(vmem_limit_bytes=60 * MIB),
        cost_estimate=pl.CostEstimate(
            flops=2 * tokens * rows * depth,
            bytes_accessed=2 * rows * depth + 2 * tokens * depth + 4 * tokens * rows,
            transcendentals=tokens * rows,
        ),
        name="student",
    )(*chunks, head, teacher)


def logit_grad_kernel(
    flags_ref, mine_ref, got_ref, scores_ref, row_s_ref, row_t_ref, weight_ref, grad_ref, cross_ref, col_ref
):
    step, last = pl.program_id(0), pl.num_programs(0) - 1
    rows = scores_ref.shape[0]
    tokens = col_ref.shape[0]
    half = rows // 2
    at = place(rows)(step)

    @pl.when(step == 0)
    def _():
        line = lax.broadcasted_iota(jnp.int32, (128, tokens), 0)
        col_ref[...] = jnp.transpose(
            jnp.where(line == 0, row_s_ref[...], jnp.where(line == 1, row_t_ref[...], weight_ref[...]))
        )

    keep = flags_ref[1] != 0
    for first in (0, half):
        part = slice(first, first + half)
        here = pl.ds(pl.multiple_of(at + first, half), half)
        cols = col_ref[here]
        student = scores_ref[part]
        target = jnp.where(keep, mine_ref[0, part], got_ref[0, part]).astype(jnp.float32)
        prob_s = jnp.exp(student - cols[:, 0:1])
        prob_t = jnp.exp(target - cols[:, 1:2])
        cross = jnp.sum(prob_t * (target - student), axis=1, keepdims=True)
        grad_ref[part] = (cols[:, 2:3] * (prob_s - prob_t)).astype(jnp.bfloat16)
        col_ref[here] = jnp.broadcast_to(cross, (half, 128))

    @pl.when(step == last)
    def _():
        cross = jnp.transpose(col_ref[...])[0:1]
        cross_ref[...] = jnp.broadcast_to(cross[None], cross_ref.shape)


def logit_grad_call(flags, mine, got, scores, total_s, total_t, weight):
    n_dp, part, rows = mine.shape
    tokens = n_dp * part
    cross = (device_count(), 1, tokens)
    whole_row = pl.BlockSpec((1, tokens), lambda k: (0, 0))
    return pl.pallas_call(
        logit_grad_kernel,
        grid=(n_dp,),
        in_specs=[
            pl.BlockSpec(memory_space=pltpu.SMEM),
            pl.BlockSpec((1, part, rows), lambda k: (k, 0, 0)),
            pl.BlockSpec((1, part, rows), lambda k: (k, 0, 0)),
            pl.BlockSpec((part, rows), lambda k: (k, 0)),
            whole_row,
            whole_row,
            whole_row,
        ],
        out_specs=[
            pl.BlockSpec((part, rows), lambda k: (k, 0)),
            pl.BlockSpec(cross, lambda k: (0, 0, 0)),
        ],
        out_shape=[
            jax.ShapeDtypeStruct((tokens, rows), jnp.bfloat16),
            jax.ShapeDtypeStruct(cross, jnp.float32),
        ],
        scratch_shapes=[pltpu.VMEM((tokens, 128), jnp.float32)],
        compiler_params=pltpu.CompilerParams(vmem_limit_bytes=24 * MIB),
        cost_estimate=pl.CostEstimate(
            flops=8 * tokens * rows, bytes_accessed=8 * tokens * rows, transcendentals=2 * tokens * rows
        ),
        name="logit_grad",
    )(flags, mine, got, scores, total_s[None], total_t[None], weight[None])


def head_grad_kernel(grad_ref, hid_ref, out_ref):
    out_ref[0] = lax.dot_general(
        grad_ref[...], hid_ref[...], (((0,), (0,)), ((), ())), preferred_element_type=jnp.float32
    ).astype(jnp.bfloat16)


def head_grad_call(logit_grad, hid):
    tokens, rows = logit_grad.shape
    depth = hid.shape[1]
    block = min(256, rows)
    return pl.pallas_call(
        head_grad_kernel,
        grid=(rows // block,),
        in_specs=[
            pl.BlockSpec((tokens, block), lambda i: (0, i)),
            pl.BlockSpec((tokens, depth), lambda i: (0, 0)),
        ],
        out_specs=pl.BlockSpec((1, block, depth), lambda i: (0, i, 0)),
        out_shape=jax.ShapeDtypeStruct((1, rows, depth), jnp.bfloat16),
        compiler_params=pltpu.CompilerParams(vmem_limit_bytes=60 * MIB),
        cost_estimate=pl.CostEstimate(
            flops=2 * tokens * rows * depth,
            bytes_accessed=2 * rows * depth + 2 * tokens * depth,
            transcendentals=0,
        ),
        name="head_grad",
    )(logit_grad, hid)


def chip_plans(n):
    def load(pair):
        ups = [sum(z < c <= p[z] for p in pair for z in range(n)) for c in range(1, n)]
        return max(ups), sum(ups)

    best = {}
    perms = list(itertools.permutations(range(n)))
    for pair in itertools.combinations_with_replacement(perms, 2):
        code = sum(3 ** (n * z + p[z]) for p in pair for z in range(n))
        if code not in best or load(pair) < load(best[code]):
            best[code] = pair
    return sorted(best.items())


def plan_tables(plans, n):
    codes = [code for code, _ in plans]
    keys = [
        (i << 8) | sum(first[z] << (2 * z) for z in range(n)) for i, (_, (first, _)) in enumerate(plans)
    ]
    pad = -len(codes) % 1024
    codes = np.array(codes + [-1] * pad, np.int32).reshape(-1, 128)
    keys = np.array(keys + [NO_PLAN] * pad, np.int32).reshape(-1, 128)
    return codes, keys


def plan_kernel(n_chips, order_ref, codes_ref, keys_ref, number_ref, flags_ref):
    chip = lax.axis_index("vocab") // 2
    code = jnp.int32(0)
    for block in range(2 * n_chips):
        dest = order_ref[block] // 2
        power = jnp.int32(0)
        for d in range(n_chips):
            power = jnp.where(dest == d, 3 ** (n_chips * (block // 2) + d), power)
        code = code + power
    key = jnp.min(jnp.where(codes_ref[...] == code, keys_ref[...], NO_PLAN))
    sends = jnp.int32(0)
    arrives = jnp.int32(0)
    for z in range(n_chips):
        goes = (key >> (2 * z)) & 3
        source = jnp.where(order_ref[2 * z] // 2 == goes, 0, 1)
        meant = jnp.where(source == 0, order_ref[2 * z], order_ref[2 * z + 1]) & 1
        sends = jnp.where(chip == z, source, sends)
        arrives = jnp.where(goes == chip, meant, arrives)
    number_ref[0] = key >> 8
    flags_ref[0] = 1 - sends
    flags_ref[1] = 1 - arrives


def plan_chips(shard_order, plans, n_chips):
    codes, keys = plan_tables(plans, n_chips)
    in_smem = pl.BlockSpec(memory_space=pltpu.SMEM)
    in_vmem = pl.BlockSpec(memory_space=pltpu.VMEM)
    return pl.pallas_call(
        functools.partial(plan_kernel, n_chips),
        in_specs=[in_smem, in_vmem, in_vmem],
        out_specs=[in_smem] * 2,
        out_shape=[jax.ShapeDtypeStruct((n,), jnp.int32) for n in (1, 2)],
        compiler_params=pltpu.CompilerParams(vmem_limit_bytes=60 * MIB),
        name="plan",
    )(shard_order, jnp.asarray(codes), jnp.asarray(keys))


def pick_kernel(flags_ref, mine_ref, other_ref, out_ref):
    dp = lax.axis_index("dp")
    n_dp, _, cols = out_ref.shape
    own = flags_ref[0] != 0
    for k in range(n_dp):
        here = pl.ds(pl.multiple_of((dp ^ k) * cols, cols), cols)
        out_ref[k] = jnp.where(own, mine_ref[:, here], other_ref[:, here])


def pick_call(flags, mine, other):
    n_dp = lax.axis_size("dp")
    shape = (n_dp, mine.shape[0], mine.shape[1] // n_dp)
    in_vmem = pl.BlockSpec(memory_space=pltpu.VMEM)
    return pl.pallas_call(
        pick_kernel,
        in_specs=[pl.BlockSpec(memory_space=pltpu.SMEM), in_vmem, in_vmem],
        out_specs=in_vmem,
        out_shape=jax.ShapeDtypeStruct(shape, jnp.bfloat16),
        compiler_params=pltpu.CompilerParams(vmem_limit_bytes=24 * MIB),
        name="pick",
    )(flags, mine, other)


def join_kernel(*refs):
    for k, ref in enumerate(refs[:-1]):
        refs[-1][k] = ref[...]


def join_call(pieces):
    in_vmem = pl.BlockSpec(memory_space=pltpu.VMEM)
    return pl.pallas_call(
        join_kernel,
        in_specs=[in_vmem] * len(pieces),
        out_specs=in_vmem,
        out_shape=jax.ShapeDtypeStruct((len(pieces), *pieces[0].shape), jnp.bfloat16),
        compiler_params=pltpu.CompilerParams(vmem_limit_bytes=24 * MIB),
        name="join",
    )(*pieces)


def over_dp(pieces):
    return [pieces[0]] + [xor_permute(pieces[k], "dp", k) for k in range(1, len(pieces))]


def wide_block(teacher, shard_order):
    token_rows = teacher.shape[0]
    n_vocab = lax.axis_size("vocab")
    piece_cols = teacher.shape[1] // n_vocab
    split_view = teacher.reshape(token_rows, n_vocab, piece_cols)
    spread_view = lax.all_to_all(split_view, "vocab", split_axis=1, concat_axis=1, tiled=True)
    ordinal = jnp.arange(n_vocab, dtype=jnp.int32)
    matches = (shard_order[None, :] == ordinal[:, None]).astype(jnp.int32)
    inverse = jnp.sum(matches * ordinal[None, :], axis=1)
    sorted_view = jnp.take(spread_view, inverse, axis=1)
    return lax.all_to_all(sorted_view, "vocab", split_axis=1, concat_axis=1, tiled=True).reshape(
        token_rows, n_vocab * piece_cols
    )


def on_device(hidden, head, teacher, shard_order, loss_weight):
    n_dp, n_vocab = lax.axis_size("dp"), lax.axis_size("vocab")
    n_chips = n_vocab // 2
    tokens = hidden.shape[0] * n_dp

    if n_chips <= 4:
        other = xor_permute(teacher, "vocab", 1)
        plans = chip_plans(n_chips)
        number, flags = plan_chips(shard_order, plans, n_chips)
        chunks = [hidden] + [xor_permute(hidden, "dp", k) for k in range(1, n_dp)]

        def over_chips(x, pair):
            pairs = [(2 * z + c, 2 * pair[c][z] + c) for z in range(n_chips) for c in range(2)]
            return lax.ppermute(x, "vocab", pairs)

        arrived = lax.switch(
            number[0],
            [functools.partial(over_chips, pair=pair) for _, pair in plans],
            pick_call(flags, teacher, other),
        )
        chunks, arrived = lax.optimization_barrier((chunks, arrived))
        pieces = over_dp([arrived[k] for k in range(n_dp)])
        student, hid, stats = student_call(chunks, head, teacher, tokens)
        pieces, stats = lax.optimization_barrier((pieces, stats))
        mine = join_call(pieces)
        got = xor_permute(mine, "vocab", 1)
    else:
        chunks = [hidden] + [xor_permute(hidden, "dp", k) for k in range(1, n_dp)]
        student, hid, stats = student_call(chunks, head, teacher, tokens)
        block = wide_block(teacher, shard_order)
        cols, dp = block.shape[1] // n_dp, lax.axis_index("dp")
        mine = jnp.stack(
            over_dp([lax.dynamic_slice_in_dim(block, (dp ^ k) * cols, cols, 1) for k in range(n_dp)])
        )
        flags, got = jnp.ones((2,), jnp.int32), mine

    total_s, total_t = combine_stats(exchange(stats), tokens)
    logit_grad, cross = logit_grad_call(flags, mine, got, student, total_s, total_t, loss_weight)
    head_grad = head_grad_call(logit_grad, hid)
    divergence = jnp.sum(exchange(cross), axis=(0, 1)) - total_t + total_s
    return head_grad, divergence


def solution(mesh):
    in_specs = (P("dp", None), P("dp", "vocab", None), P("dp", "vocab"), P(), P())
    out_specs = (P("dp", "vocab", None), P())
    return jax.shard_map(
        on_device, mesh=mesh, in_specs=in_specs, out_specs=out_specs, check_vma=False
    )
```

```python
import functools
import itertools

import jax
import jax.numpy as jnp
import numpy as np
from jax import lax
from jax.experimental import pallas as pl
from jax.experimental.pallas import tpu as pltpu
from jax.sharding import PartitionSpec as P

MIB = 1024 * 1024
LOWEST = float(np.finfo(np.float32).min)
NO_PLAN = 2**30


def xor_permute(x, axis, k):
    size = lax.axis_size(axis)
    return lax.ppermute(x, axis, [(i, i ^ k) for i in range(size)])


def device_count():
    return lax.axis_size("dp") * lax.axis_size("vocab")


def exchange(copies):
    return lax.all_to_all(copies, ("dp", "vocab"), split_axis=0, concat_axis=0, tiled=True)


def log_sum_exp(parts, axis):
    top = jnp.max(parts, axis=axis, keepdims=True)
    total = jnp.sum(jnp.exp(parts - top), axis=axis, keepdims=True)
    return jnp.squeeze(top + jnp.log(total), axis)


def combine_stats(parts, tokens):
    n_dp, n_vocab = lax.axis_size("dp"), lax.axis_size("vocab")
    student = log_sum_exp(parts[:, 0, :tokens], 0)
    target = log_sum_exp(parts[:, 0, tokens:].reshape(n_dp, n_vocab, tokens // n_dp), 1)
    return student, target.reshape(tokens)


def place(rows):
    return lambda k: pl.multiple_of((lax.axis_index("dp") ^ k) * rows, rows)


def student_kernel(n_chunks, *refs):
    chunk_refs = refs[:n_chunks]
    head_ref, teacher_ref, out_ref, hid_out_ref, stats_ref = refs[n_chunks : n_chunks + 5]
    hid_ref, rows_ref, logits_ref, scores_ref, top_ref, sum_ref, stat_ref = refs[n_chunks + 5 : -4]
    chunk_sems, head_sems, out_sems, sems = refs[-4:]
    tokens, rows = scores_ref.shape
    own = teacher_ref.shape[0]
    block = min(256, rows)
    blocks = rows // block

    def head_copy(i):
        here = pl.ds(pl.multiple_of(i * block, block), block)
        return pltpu.make_async_copy(head_ref.at[0, here], rows_ref.at[here], head_sems.at[i])

    def out_copy(i):
        here = pl.ds(pl.multiple_of(i * block, block), block)
        return pltpu.make_async_copy(scores_ref.at[:, here], out_ref.at[:, here], out_sems.at[i])

    teacher_copy = pltpu.make_async_copy(teacher_ref, logits_ref, sems.at[0])
    hid_copy = pltpu.make_async_copy(hid_ref, hid_out_ref, sems.at[1])
    copies = []
    for k, ref in enumerate(chunk_refs):
        copies.append(
            pltpu.make_async_copy(ref, hid_ref.at[k * own : (k + 1) * own], chunk_sems.at[k])
        )
    teacher_copy.start()
    for copy in copies:
        copy.start()
    for i in range(blocks):
        head_copy(i).start()

    top_ref[...] = jnp.full(top_ref.shape, LOWEST, jnp.float32)
    sum_ref[...] = jnp.zeros(sum_ref.shape, jnp.float32)
    teacher_copy.wait()
    values = logits_ref[...].astype(jnp.float32)
    top = jnp.max(values, axis=1, keepdims=True)
    total = jnp.sum(jnp.exp(values - top), axis=1, keepdims=True)
    stat = jnp.transpose(jnp.broadcast_to(top + jnp.log(total), (own, 128)))[0:1]
    stats_ref[:, :, tokens:] = jnp.broadcast_to(stat[None], (stats_ref.shape[0], 1, own))
    for copy in copies:
        copy.wait()
    hid_copy.start()

    def scores_of(i):
        columns = pl.ds(pl.multiple_of(i * block, block), block)
        scores_ref[:, columns] = lax.dot_general(
            hid_ref[...], rows_ref[columns], (((1,), (1,)), ((), ())), preferred_element_type=jnp.float32
        )

    def stats_of(i):
        values = scores_ref[:, pl.ds(pl.multiple_of(i * block, block), block)]
        old = top_ref[...]
        top = jnp.maximum(old, jnp.max(values, axis=1, keepdims=True))
        total = jnp.sum(jnp.exp(values - top), axis=1, keepdims=True)
        top_ref[...] = top
        sum_ref[...] = sum_ref[...] * jnp.exp(old - top) + total

    def step(i, carry):
        head_copy(i).wait()
        stats_of(i - 1)
        scores_of(i)
        out_copy(i - 1).start()
        return carry

    head_copy(0).wait()
    scores_of(0)
    lax.fori_loop(1, blocks, step, 0)
    out_copy(blocks - 1).start()
    stats_of(blocks - 1)
    at = place(own)
    for k in range(n_chunks):
        here = slice(k * own, (k + 1) * own)
        stat = top_ref[here] + jnp.log(sum_ref[here])
        stat_ref[pl.ds(at(k), own)] = jnp.broadcast_to(stat, (own, 128))
    stat = jnp.transpose(stat_ref[...])[0:1]
    stats_ref[:, :, :tokens] = jnp.broadcast_to(stat[None], (stats_ref.shape[0], 1, tokens))
    for i in range(blocks):
        out_copy(i).wait()
    hid_copy.wait()


def student_call(chunks, head, teacher, tokens):
    _, rows, depth = head.shape
    blocks = rows // min(256, rows)
    in_hbm = pl.BlockSpec(memory_space=pltpu.HBM)
    return pl.pallas_call(
        functools.partial(student_kernel, len(chunks)),
        in_specs=[in_hbm] * (len(chunks) + 2),
        out_specs=[in_hbm, in_hbm, pl.BlockSpec(memory_space=pltpu.VMEM)],
        out_shape=[
            jax.ShapeDtypeStruct((tokens, rows), jnp.float32),
            jax.ShapeDtypeStruct((tokens, depth), jnp.bfloat16),
            jax.ShapeDtypeStruct((device_count(), 1, tokens + teacher.shape[0]), jnp.float32),
        ],
        scratch_shapes=[
            pltpu.VMEM((tokens, depth), jnp.bfloat16),
            pltpu.VMEM((rows, depth), jnp.bfloat16),
            pltpu.VMEM(teacher.shape, jnp.bfloat16),
            pltpu.VMEM((tokens, rows), jnp.float32),
            pltpu.VMEM((tokens, 1), jnp.float32),
            pltpu.VMEM((tokens, 1), jnp.float32),
            pltpu.VMEM((tokens, 128), jnp.float32),
            pltpu.SemaphoreType.DMA((len(chunks),)),
            pltpu.SemaphoreType.DMA((blocks,)),
            pltpu.SemaphoreType.DMA((blocks,)),
            pltpu.SemaphoreType.DMA((2,)),
        ],
        compiler_params=pltpu.CompilerParams(vmem_limit_bytes=60 * MIB),
        cost_estimate=pl.CostEstimate(
            flops=2 * tokens * rows * depth,
            bytes_accessed=2 * rows * depth + 2 * tokens * depth + 4 * tokens * rows,
            transcendentals=tokens * rows,
        ),
        name="student",
    )(*chunks, head, teacher)


def logit_grad_kernel(
    flags_ref, mine_ref, got_ref, scores_in_ref, row_s_ref, row_t_ref, weight_ref, out_ref, cross_ref,
    target_ref, scores_ref, grad_ref, col_ref, target_sems, scores_sems, out_sems,
):
    n_dp, rows, _ = target_ref.shape
    tokens = n_dp * rows
    half = rows // 2
    at = place(rows)

    def piece(k):
        return pl.ds(pl.multiple_of(k * rows, rows), rows)

    def target_copy(ref, k):
        return pltpu.make_async_copy(ref.at[k], target_ref.at[k], target_sems.at[k])

    def scores_copy(k):
        return pltpu.make_async_copy(
            scores_in_ref.at[piece(k)], scores_ref.at[piece(k)], scores_sems.at[k]
        )

    def out_copy(k):
        return pltpu.make_async_copy(grad_ref.at[piece(k)], out_ref.at[piece(k)], out_sems.at[k])

    for k in range(n_dp):
        scores_copy(k).start()

        @pl.when(flags_ref[1] != 0)
        def _():
            target_copy(mine_ref, k).start()

        @pl.when(flags_ref[1] == 0)
        def _():
            target_copy(got_ref, k).start()

    line = lax.broadcasted_iota(jnp.int32, (128, tokens), 0)
    col_ref[...] = jnp.transpose(
        jnp.where(line == 0, row_s_ref[...], jnp.where(line == 1, row_t_ref[...], weight_ref[...]))
    )

    def step(k, carry):
        scores_copy(k).wait()
        target_copy(mine_ref, k).wait()
        for first in (0, half):
            here = pl.ds(pl.multiple_of(at(k) + first, half), half)
            part = pl.ds(pl.multiple_of(k * rows + first, half), half)
            cols = col_ref[here]
            student = scores_ref[part]
            target = target_ref[k, first : first + half].astype(jnp.float32)
            prob_s = jnp.exp(student - cols[:, 0:1])
            prob_t = jnp.exp(target - cols[:, 1:2])
            cross = jnp.sum(prob_t * (target - student), axis=1, keepdims=True)
            grad_ref[part] = (cols[:, 2:3] * (prob_s - prob_t)).astype(jnp.bfloat16)
            col_ref[here] = jnp.broadcast_to(cross, (half, 128))
        out_copy(k).start()
        return carry

    lax.fori_loop(0, n_dp, step, 0)
    cross = jnp.transpose(col_ref[...])[0:1]
    cross_ref[...] = jnp.broadcast_to(cross[None], cross_ref.shape)
    for k in range(n_dp):
        out_copy(k).wait()


def logit_grad_call(flags, mine, got, scores, total_s, total_t, weight):
    n_dp, part, rows = mine.shape
    tokens = n_dp * part
    in_hbm = pl.BlockSpec(memory_space=pltpu.HBM)
    in_vmem = pl.BlockSpec(memory_space=pltpu.VMEM)
    return pl.pallas_call(
        logit_grad_kernel,
        in_specs=[pl.BlockSpec(memory_space=pltpu.SMEM)] + [in_hbm] * 3 + [in_vmem] * 3,
        out_specs=[in_hbm, in_vmem],
        out_shape=[
            jax.ShapeDtypeStruct((tokens, rows), jnp.bfloat16),
            jax.ShapeDtypeStruct((device_count(), 1, tokens), jnp.float32),
        ],
        scratch_shapes=[
            pltpu.VMEM(mine.shape, jnp.bfloat16),
            pltpu.VMEM((tokens, rows), jnp.float32),
            pltpu.VMEM((tokens, rows), jnp.bfloat16),
            pltpu.VMEM((tokens, 128), jnp.float32),
            pltpu.SemaphoreType.DMA((n_dp,)),
            pltpu.SemaphoreType.DMA((n_dp,)),
            pltpu.SemaphoreType.DMA((n_dp,)),
        ],
        compiler_params=pltpu.CompilerParams(vmem_limit_bytes=60 * MIB),
        cost_estimate=pl.CostEstimate(
            flops=8 * tokens * rows, bytes_accessed=8 * tokens * rows, transcendentals=2 * tokens * rows
        ),
        name="logit_grad",
    )(flags, mine, got, scores, total_s[None], total_t[None], weight[None])


def head_grad_kernel(grad_ref, hid_ref, out_ref, turned_ref):
    @pl.when(pl.program_id(0) == 0)
    def _():
        turned_ref[...] = jnp.transpose(grad_ref[...])

    out_ref[0] = jnp.dot(
        turned_ref[...], hid_ref[...], preferred_element_type=jnp.float32
    ).astype(jnp.bfloat16)


def head_grad_call(logit_grad, hid):
    tokens, rows = logit_grad.shape
    depth = hid.shape[1]
    block = 512
    return pl.pallas_call(
        head_grad_kernel,
        grid=(depth // block,),
        in_specs=[
            pl.BlockSpec((tokens, rows), lambda i: (0, 0)),
            pl.BlockSpec((tokens, block), lambda i: (0, i)),
        ],
        out_specs=pl.BlockSpec((1, rows, block), lambda i: (0, 0, i)),
        out_shape=jax.ShapeDtypeStruct((1, rows, depth), jnp.bfloat16),
        scratch_shapes=[pltpu.VMEM((rows, tokens), jnp.bfloat16)],
        compiler_params=pltpu.CompilerParams(vmem_limit_bytes=60 * MIB),
        cost_estimate=pl.CostEstimate(
            flops=2 * tokens * rows * depth,
            bytes_accessed=2 * rows * depth + 2 * tokens * depth,
            transcendentals=0,
        ),
        name="head_grad",
    )(logit_grad, hid)


def chip_plans(n):
    def load(pair):
        ups = [sum(z < c <= p[z] for p in pair for z in range(n)) for c in range(1, n)]
        return max(ups), sum(ups)

    best = {}
    perms = list(itertools.permutations(range(n)))
    for pair in itertools.combinations_with_replacement(perms, 2):
        code = sum(3 ** (n * z + p[z]) for p in pair for z in range(n))
        if code not in best or load(pair) < load(best[code]):
            best[code] = pair
    return sorted(best.items())


def plan_tables(plans, n):
    codes = [code for code, _ in plans]
    keys = [
        (i << 8) | sum(first[z] << (2 * z) for z in range(n)) for i, (_, (first, _)) in enumerate(plans)
    ]
    pad = -len(codes) % 1024
    codes = np.array(codes + [-1] * pad, np.int32).reshape(-1, 128)
    keys = np.array(keys + [NO_PLAN] * pad, np.int32).reshape(-1, 128)
    return codes, keys


def plan_kernel(n_chips, order_ref, codes_ref, keys_ref, number_ref, flags_ref):
    chip = lax.axis_index("vocab") // 2
    code = jnp.int32(0)
    for block in range(2 * n_chips):
        dest = order_ref[block] // 2
        power = jnp.int32(0)
        for d in range(n_chips):
            power = jnp.where(dest == d, 3 ** (n_chips * (block // 2) + d), power)
        code = code + power
    key = jnp.min(jnp.where(codes_ref[...] == code, keys_ref[...], NO_PLAN))
    sends = jnp.int32(0)
    arrives = jnp.int32(0)
    for z in range(n_chips):
        goes = (key >> (2 * z)) & 3
        source = jnp.where(order_ref[2 * z] // 2 == goes, 0, 1)
        meant = jnp.where(source == 0, order_ref[2 * z], order_ref[2 * z + 1]) & 1
        sends = jnp.where(chip == z, source, sends)
        arrives = jnp.where(goes == chip, meant, arrives)
    number_ref[0] = key >> 8
    flags_ref[0] = 1 - sends
    flags_ref[1] = 1 - arrives


def plan_chips(shard_order, plans, n_chips):
    codes, keys = plan_tables(plans, n_chips)
    in_smem = pl.BlockSpec(memory_space=pltpu.SMEM)
    in_vmem = pl.BlockSpec(memory_space=pltpu.VMEM)
    return pl.pallas_call(
        functools.partial(plan_kernel, n_chips),
        in_specs=[in_smem, in_vmem, in_vmem],
        out_specs=[in_smem] * 2,
        out_shape=[jax.ShapeDtypeStruct((n,), jnp.int32) for n in (1, 2)],
        compiler_params=pltpu.CompilerParams(vmem_limit_bytes=60 * MIB),
        name="plan",
    )(shard_order, jnp.asarray(codes), jnp.asarray(keys))


def pick_kernel(flags_ref, mine_ref, other_ref, out_ref):
    dp = lax.axis_index("dp")
    n_dp, _, cols = out_ref.shape
    own = flags_ref[0] != 0
    for k in range(n_dp):
        here = pl.ds(pl.multiple_of((dp ^ k) * cols, cols), cols)
        out_ref[k] = jnp.where(own, mine_ref[:, here], other_ref[:, here])


def pick_call(flags, mine, other):
    n_dp = lax.axis_size("dp")
    shape = (n_dp, mine.shape[0], mine.shape[1] // n_dp)
    in_vmem = pl.BlockSpec(memory_space=pltpu.VMEM)
    return pl.pallas_call(
        pick_kernel,
        in_specs=[pl.BlockSpec(memory_space=pltpu.SMEM), in_vmem, in_vmem],
        out_specs=in_vmem,
        out_shape=jax.ShapeDtypeStruct(shape, jnp.bfloat16),
        compiler_params=pltpu.CompilerParams(vmem_limit_bytes=24 * MIB),
        name="pick",
    )(flags, mine, other)


def join_kernel(*refs):
    for k, ref in enumerate(refs[:-1]):
        refs[-1][k] = ref[...]


def join_call(pieces):
    in_vmem = pl.BlockSpec(memory_space=pltpu.VMEM)
    return pl.pallas_call(
        join_kernel,
        in_specs=[in_vmem] * len(pieces),
        out_specs=in_vmem,
        out_shape=jax.ShapeDtypeStruct((len(pieces), *pieces[0].shape), jnp.bfloat16),
        compiler_params=pltpu.CompilerParams(vmem_limit_bytes=24 * MIB),
        name="join",
    )(*pieces)


def over_dp(pieces):
    return [pieces[0]] + [xor_permute(pieces[k], "dp", k) for k in range(1, len(pieces))]


def wide_block(teacher, shard_order):
    token_rows = teacher.shape[0]
    n_vocab = lax.axis_size("vocab")
    piece_cols = teacher.shape[1] // n_vocab
    split_view = teacher.reshape(token_rows, n_vocab, piece_cols)
    spread_view = lax.all_to_all(split_view, "vocab", split_axis=1, concat_axis=1, tiled=True)
    ordinal = jnp.arange(n_vocab, dtype=jnp.int32)
    matches = (shard_order[None, :] == ordinal[:, None]).astype(jnp.int32)
    inverse = jnp.sum(matches * ordinal[None, :], axis=1)
    sorted_view = jnp.take(spread_view, inverse, axis=1)
    return lax.all_to_all(sorted_view, "vocab", split_axis=1, concat_axis=1, tiled=True).reshape(
        token_rows, n_vocab * piece_cols
    )


def on_device(hidden, head, teacher, shard_order, loss_weight):
    n_dp, n_vocab = lax.axis_size("dp"), lax.axis_size("vocab")
    n_chips = n_vocab // 2
    tokens = hidden.shape[0] * n_dp

    if n_chips <= 4:
        other = xor_permute(teacher, "vocab", 1)
        plans = chip_plans(n_chips)
        number, flags = plan_chips(shard_order, plans, n_chips)
        chunks = [hidden] + [xor_permute(hidden, "dp", k) for k in range(1, n_dp)]

        def over_chips(x, pair):
            pairs = [(2 * z + c, 2 * pair[c][z] + c) for z in range(n_chips) for c in range(2)]
            return lax.ppermute(x, "vocab", pairs)

        arrived = lax.switch(
            number[0],
            [functools.partial(over_chips, pair=pair) for _, pair in plans],
            pick_call(flags, teacher, other),
        )
        chunks, arrived = lax.optimization_barrier((chunks, arrived))
        pieces = over_dp([arrived[k] for k in range(n_dp)])
        student, hid, stats = student_call(chunks, head, teacher, tokens)
        pieces, stats = lax.optimization_barrier((pieces, stats))
        mine = join_call(pieces)
        got = xor_permute(mine, "vocab", 1)
    else:
        chunks = [hidden] + [xor_permute(hidden, "dp", k) for k in range(1, n_dp)]
        student, hid, stats = student_call(chunks, head, teacher, tokens)
        block = wide_block(teacher, shard_order)
        cols, dp = block.shape[1] // n_dp, lax.axis_index("dp")
        mine = jnp.stack(
            over_dp([lax.dynamic_slice_in_dim(block, (dp ^ k) * cols, cols, 1) for k in range(n_dp)])
        )
        flags, got = jnp.ones((2,), jnp.int32), mine

    total_s, total_t = combine_stats(exchange(stats), tokens)
    logit_grad, cross = logit_grad_call(flags, mine, got, student, total_s, total_t, loss_weight)
    head_grad = head_grad_call(logit_grad, hid)
    divergence = jnp.sum(exchange(cross), axis=(0, 1)) - total_t + total_s
    return head_grad, divergence


def solution(mesh):
    in_specs = (P("dp", None), P("dp", "vocab", None), P("dp", "vocab"), P(), P())
    out_specs = (P("dp", "vocab", None), P())
    return jax.shard_map(
        on_device, mesh=mesh, in_specs=in_specs, out_specs=out_specs, check_vma=False
    )
```

```python
import functools
import itertools

import jax
import jax.numpy as jnp
import numpy as np
from jax import lax
from jax.experimental import pallas as pl
from jax.experimental.pallas import tpu as pltpu
from jax.sharding import PartitionSpec as P

MIB = 1024 * 1024
LOWEST = float(np.finfo(np.float32).min)
NO_PLAN = 2**30


def xor_permute(x, axis, k):
    size = lax.axis_size(axis)
    return lax.ppermute(x, axis, [(i, i ^ k) for i in range(size)])


def device_count():
    return lax.axis_size("dp") * lax.axis_size("vocab")


def exchange(copies):
    return lax.all_to_all(copies, ("dp", "vocab"), split_axis=0, concat_axis=0, tiled=True)


def log_sum_exp(parts, axis):
    top = jnp.max(parts, axis=axis, keepdims=True)
    total = jnp.sum(jnp.exp(parts - top), axis=axis, keepdims=True)
    return jnp.squeeze(top + jnp.log(total), axis)


def combine_stats(parts, tokens):
    n_dp, n_vocab = lax.axis_size("dp"), lax.axis_size("vocab")
    student = log_sum_exp(parts[:, 0, :tokens], 0)
    target = log_sum_exp(parts[:, 0, tokens:].reshape(n_dp, n_vocab, tokens // n_dp), 1)
    return student, target.reshape(tokens)


def place(rows):
    return lambda k: pl.multiple_of((lax.axis_index("dp") ^ k) * rows, rows)


def student_kernel(n_chunks, *refs):
    chunk_refs = refs[:n_chunks]
    head_ref, teacher_ref, out_ref, hid_out_ref, stats_ref = refs[n_chunks : n_chunks + 5]
    hid_ref, rows_ref, logits_ref, scores_ref, top_ref, sum_ref, stat_ref = refs[n_chunks + 5 : -4]
    chunk_sems, head_sems, out_sems, sems = refs[-4:]
    tokens, rows = scores_ref.shape
    own = teacher_ref.shape[0]
    block = min(256, rows)
    blocks = rows // block

    def head_copy(i):
        here = pl.ds(pl.multiple_of(i * block, block), block)
        return pltpu.make_async_copy(head_ref.at[0, here], rows_ref.at[here], head_sems.at[i])

    def out_copy(i):
        here = pl.ds(pl.multiple_of(i * block, block), block)
        return pltpu.make_async_copy(scores_ref.at[:, here], out_ref.at[:, here], out_sems.at[i])

    teacher_copy = pltpu.make_async_copy(teacher_ref, logits_ref, sems.at[0])
    hid_copy = pltpu.make_async_copy(hid_ref, hid_out_ref, sems.at[1])
    copies = []
    for k, ref in enumerate(chunk_refs):
        copies.append(
            pltpu.make_async_copy(ref, hid_ref.at[k * own : (k + 1) * own], chunk_sems.at[k])
        )
    teacher_copy.start()
    for copy in copies:
        copy.start()
    for i in range(blocks):
        head_copy(i).start()

    top_ref[...] = jnp.full(top_ref.shape, LOWEST, jnp.float32)
    sum_ref[...] = jnp.zeros(sum_ref.shape, jnp.float32)
    teacher_copy.wait()
    values = logits_ref[...].astype(jnp.float32)
    top = jnp.max(values, axis=1, keepdims=True)
    total = jnp.sum(jnp.exp(values - top), axis=1, keepdims=True)
    stat = jnp.transpose(jnp.broadcast_to(top + jnp.log(total), (own, 128)))[0:1]
    stats_ref[:, :, tokens:] = jnp.broadcast_to(stat[None], (stats_ref.shape[0], 1, own))
    for copy in copies:
        copy.wait()
    hid_copy.start()

    def scores_of(i):
        columns = pl.ds(pl.multiple_of(i * block, block), block)
        scores_ref[:, columns] = lax.dot_general(
            hid_ref[...], rows_ref[columns], (((1,), (1,)), ((), ())), preferred_element_type=jnp.float32
        )

    def stats_of(i):
        values = scores_ref[:, pl.ds(pl.multiple_of(i * block, block), block)]
        old = top_ref[...]
        top = jnp.maximum(old, jnp.max(values, axis=1, keepdims=True))
        total = jnp.sum(jnp.exp(values - top), axis=1, keepdims=True)
        top_ref[...] = top
        sum_ref[...] = sum_ref[...] * jnp.exp(old - top) + total

    def step(i, carry):
        head_copy(i).wait()
        stats_of(i - 1)
        scores_of(i)
        out_copy(i - 1).start()
        return carry

    head_copy(0).wait()
    scores_of(0)
    lax.fori_loop(1, blocks, step, 0)
    out_copy(blocks - 1).start()
    stats_of(blocks - 1)
    at = place(own)
    for k in range(n_chunks):
        here = slice(k * own, (k + 1) * own)
        stat = top_ref[here] + jnp.log(sum_ref[here])
        stat_ref[pl.ds(at(k), own)] = jnp.broadcast_to(stat, (own, 128))
    stat = jnp.transpose(stat_ref[...])[0:1]
    stats_ref[:, :, :tokens] = jnp.broadcast_to(stat[None], (stats_ref.shape[0], 1, tokens))
    for i in range(blocks):
        out_copy(i).wait()
    hid_copy.wait()


def student_call(chunks, head, teacher, tokens):
    _, rows, depth = head.shape
    blocks = rows // min(256, rows)
    in_hbm = pl.BlockSpec(memory_space=pltpu.HBM)
    return pl.pallas_call(
        functools.partial(student_kernel, len(chunks)),
        in_specs=[in_hbm] * (len(chunks) + 2),
        out_specs=[in_hbm, in_hbm, pl.BlockSpec(memory_space=pltpu.VMEM)],
        out_shape=[
            jax.ShapeDtypeStruct((tokens, rows), jnp.float32),
            jax.ShapeDtypeStruct((tokens, depth), jnp.bfloat16),
            jax.ShapeDtypeStruct((device_count(), 1, tokens + teacher.shape[0]), jnp.float32),
        ],
        scratch_shapes=[
            pltpu.VMEM((tokens, depth), jnp.bfloat16),
            pltpu.VMEM((rows, depth), jnp.bfloat16),
            pltpu.VMEM(teacher.shape, jnp.bfloat16),
            pltpu.VMEM((tokens, rows), jnp.float32),
            pltpu.VMEM((tokens, 1), jnp.float32),
            pltpu.VMEM((tokens, 1), jnp.float32),
            pltpu.VMEM((tokens, 128), jnp.float32),
            pltpu.SemaphoreType.DMA((len(chunks),)),
            pltpu.SemaphoreType.DMA((blocks,)),
            pltpu.SemaphoreType.DMA((blocks,)),
            pltpu.SemaphoreType.DMA((2,)),
        ],
        compiler_params=pltpu.CompilerParams(vmem_limit_bytes=60 * MIB),
        cost_estimate=pl.CostEstimate(
            flops=2 * tokens * rows * depth,
            bytes_accessed=2 * rows * depth + 2 * tokens * depth + 4 * tokens * rows,
            transcendentals=tokens * rows,
        ),
        name="student",
    )(*chunks, head, teacher)


def cross_kernel(flags_ref, mine_ref, got_ref, scores_ref, out_ref, col_ref):
    step, last = pl.program_id(0), pl.num_programs(0) - 1
    rows = scores_ref.shape[0]
    tokens = col_ref.shape[0]
    half = rows // 2
    at = place(rows)(step)
    keep = flags_ref[1] != 0
    lane = lax.broadcasted_iota(jnp.int32, (half, 128), 1)
    for first in (0, half):
        part = slice(first, first + half)
        here = pl.ds(pl.multiple_of(at + first, half), half)
        target = jnp.where(keep, mine_ref[0, part], got_ref[0, part]).astype(jnp.float32)
        top = jnp.max(target, axis=1, keepdims=True)
        cross = jnp.exp(target - top) * (target - scores_ref[part])
        col_ref[here] = jnp.where(lane == 0, top, jnp.sum(cross, axis=1, keepdims=True))

    @pl.when(step == last)
    def _():
        lines = jnp.transpose(col_ref[...])
        for i in range(2):
            line = jnp.broadcast_to(lines[i : i + 1][None], (out_ref.shape[0], 1, tokens))
            out_ref[:, :, i * tokens : (i + 1) * tokens] = line


def block_specs(n_dp, part, rows):
    return [
        pl.BlockSpec(memory_space=pltpu.SMEM),
        pl.BlockSpec((1, part, rows), lambda k: (k, 0, 0)),
        pl.BlockSpec((1, part, rows), lambda k: (k, 0, 0)),
        pl.BlockSpec((part, rows), lambda k: (k, 0)),
    ]


def cross_call(flags, mine, got, scores):
    n_dp, part, rows = mine.shape
    tokens = n_dp * part
    shape = (device_count(), 1, 2 * tokens)
    return pl.pallas_call(
        cross_kernel,
        grid=(n_dp,),
        in_specs=block_specs(n_dp, part, rows),
        out_specs=pl.BlockSpec(shape, lambda k: (0, 0, 0)),
        out_shape=jax.ShapeDtypeStruct(shape, jnp.float32),
        scratch_shapes=[pltpu.VMEM((tokens, 128), jnp.float32)],
        compiler_params=pltpu.CompilerParams(vmem_limit_bytes=24 * MIB),
        cost_estimate=pl.CostEstimate(
            flops=5 * tokens * rows, bytes_accessed=8 * tokens * rows, transcendentals=tokens * rows
        ),
        name="cross",
    )(flags, mine, got, scores)


def logit_grad_kernel(
    flags_ref, mine_ref, got_ref, scores_ref, row_s_ref, row_t_ref, weight_ref, grad_ref, col_ref
):
    step = pl.program_id(0)
    rows = scores_ref.shape[0]
    tokens = col_ref.shape[0]
    half = rows // 2
    at = place(rows)(step)

    @pl.when(step == 0)
    def _():
        line = lax.broadcasted_iota(jnp.int32, (128, tokens), 0)
        col_ref[...] = jnp.transpose(
            jnp.where(line == 0, row_s_ref[...], jnp.where(line == 1, row_t_ref[...], weight_ref[...]))
        )

    keep = flags_ref[1] != 0
    for first in (0, half):
        part = slice(first, first + half)
        cols = col_ref[pl.ds(pl.multiple_of(at + first, half), half)]
        target = jnp.where(keep, mine_ref[0, part], got_ref[0, part]).astype(jnp.float32)
        prob_s = jnp.exp(scores_ref[part] - cols[:, 0:1])
        prob_t = jnp.exp(target - cols[:, 1:2])
        grad_ref[part] = (cols[:, 2:3] * (prob_s - prob_t)).astype(jnp.bfloat16)


def logit_grad_call(flags, mine, got, scores, total_s, total_t, weight):
    n_dp, part, rows = mine.shape
    tokens = n_dp * part
    whole_row = pl.BlockSpec((1, tokens), lambda k: (0, 0))
    return pl.pallas_call(
        logit_grad_kernel,
        grid=(n_dp,),
        in_specs=block_specs(n_dp, part, rows) + [whole_row] * 3,
        out_specs=pl.BlockSpec((part, rows), lambda k: (k, 0)),
        out_shape=jax.ShapeDtypeStruct((tokens, rows), jnp.bfloat16),
        scratch_shapes=[pltpu.VMEM((tokens, 128), jnp.float32)],
        compiler_params=pltpu.CompilerParams(vmem_limit_bytes=24 * MIB),
        cost_estimate=pl.CostEstimate(
            flops=4 * tokens * rows, bytes_accessed=8 * tokens * rows, transcendentals=2 * tokens * rows
        ),
        name="logit_grad",
    )(flags, mine, got, scores, total_s[None], total_t[None], weight[None])


def head_grad_kernel(grad_ref, hid_ref, out_ref):
    out_ref[0] = lax.dot_general(
        grad_ref[...], hid_ref[...], (((0,), (0,)), ((), ())), preferred_element_type=jnp.float32
    ).astype(jnp.bfloat16)


def head_grad_call(logit_grad, hid):
    tokens, rows = logit_grad.shape
    depth = hid.shape[1]
    block = min(256, rows)
    return pl.pallas_call(
        head_grad_kernel,
        grid=(rows // block,),
        in_specs=[
            pl.BlockSpec((tokens, block), lambda i: (0, i)),
            pl.BlockSpec((tokens, depth), lambda i: (0, 0)),
        ],
        out_specs=pl.BlockSpec((1, block, depth), lambda i: (0, i, 0)),
        out_shape=jax.ShapeDtypeStruct((1, rows, depth), jnp.bfloat16),
        compiler_params=pltpu.CompilerParams(vmem_limit_bytes=60 * MIB),
        cost_estimate=pl.CostEstimate(
            flops=2 * tokens * rows * depth,
            bytes_accessed=2 * rows * depth + 2 * tokens * depth,
            transcendentals=0,
        ),
        name="head_grad",
    )(logit_grad, hid)


def chip_plans(n):
    def load(pair):
        ups = [sum(z < c <= p[z] for p in pair for z in range(n)) for c in range(1, n)]
        return max(ups), sum(ups)

    best = {}
    perms = list(itertools.permutations(range(n)))
    for pair in itertools.combinations_with_replacement(perms, 2):
        code = sum(3 ** (n * z + p[z]) for p in pair for z in range(n))
        if code not in best or load(pair) < load(best[code]):
            best[code] = pair
    return sorted(best.items())


def plan_tables(plans, n):
    codes = [code for code, _ in plans]
    keys = [
        (i << 8) | sum(first[z] << (2 * z) for z in range(n)) for i, (_, (first, _)) in enumerate(plans)
    ]
    pad = -len(codes) % 1024
    codes = np.array(codes + [-1] * pad, np.int32).reshape(-1, 128)
    keys = np.array(keys + [NO_PLAN] * pad, np.int32).reshape(-1, 128)
    return codes, keys


def plan_kernel(n_chips, order_ref, codes_ref, keys_ref, number_ref, flags_ref):
    chip = lax.axis_index("vocab") // 2
    code = jnp.int32(0)
    for block in range(2 * n_chips):
        dest = order_ref[block] // 2
        power = jnp.int32(0)
        for d in range(n_chips):
            power = jnp.where(dest == d, 3 ** (n_chips * (block // 2) + d), power)
        code = code + power
    key = jnp.min(jnp.where(codes_ref[...] == code, keys_ref[...], NO_PLAN))
    sends = jnp.int32(0)
    arrives = jnp.int32(0)
    for z in range(n_chips):
        goes = (key >> (2 * z)) & 3
        source = jnp.where(order_ref[2 * z] // 2 == goes, 0, 1)
        meant = jnp.where(source == 0, order_ref[2 * z], order_ref[2 * z + 1]) & 1
        sends = jnp.where(chip == z, source, sends)
        arrives = jnp.where(goes == chip, meant, arrives)
    number_ref[0] = key >> 8
    flags_ref[0] = 1 - sends
    flags_ref[1] = 1 - arrives


def plan_chips(shard_order, plans, n_chips):
    codes, keys = plan_tables(plans, n_chips)
    in_smem = pl.BlockSpec(memory_space=pltpu.SMEM)
    in_vmem = pl.BlockSpec(memory_space=pltpu.VMEM)
    return pl.pallas_call(
        functools.partial(plan_kernel, n_chips),
        in_specs=[in_smem, in_vmem, in_vmem],
        out_specs=[in_smem] * 2,
        out_shape=[jax.ShapeDtypeStruct((n,), jnp.int32) for n in (1, 2)],
        compiler_params=pltpu.CompilerParams(vmem_limit_bytes=60 * MIB),
        name="plan",
    )(shard_order, jnp.asarray(codes), jnp.asarray(keys))


def pick_kernel(flags_ref, mine_ref, other_ref, out_ref):
    dp = lax.axis_index("dp")
    n_dp, _, cols = out_ref.shape
    own = flags_ref[0] != 0
    for k in range(n_dp):
        here = pl.ds(pl.multiple_of((dp ^ k) * cols, cols), cols)
        out_ref[k] = jnp.where(own, mine_ref[:, here], other_ref[:, here])


def pick_call(flags, mine, other):
    n_dp = lax.axis_size("dp")
    shape = (n_dp, mine.shape[0], mine.shape[1] // n_dp)
    in_vmem = pl.BlockSpec(memory_space=pltpu.VMEM)
    return pl.pallas_call(
        pick_kernel,
        in_specs=[pl.BlockSpec(memory_space=pltpu.SMEM), in_vmem, in_vmem],
        out_specs=in_vmem,
        out_shape=jax.ShapeDtypeStruct(shape, jnp.bfloat16),
        compiler_params=pltpu.CompilerParams(vmem_limit_bytes=24 * MIB),
        name="pick",
    )(flags, mine, other)


def join_kernel(*refs):
    for k, ref in enumerate(refs[:-1]):
        refs[-1][k] = ref[...]


def join_call(pieces):
    in_vmem = pl.BlockSpec(memory_space=pltpu.VMEM)
    return pl.pallas_call(
        join_kernel,
        in_specs=[in_vmem] * len(pieces),
        out_specs=in_vmem,
        out_shape=jax.ShapeDtypeStruct((len(pieces), *pieces[0].shape), jnp.bfloat16),
        compiler_params=pltpu.CompilerParams(vmem_limit_bytes=24 * MIB),
        name="join",
    )(*pieces)


def over_dp(pieces):
    return [pieces[0]] + [xor_permute(pieces[k], "dp", k) for k in range(1, len(pieces))]


def wide_block(teacher, shard_order):
    token_rows = teacher.shape[0]
    n_vocab = lax.axis_size("vocab")
    piece_cols = teacher.shape[1] // n_vocab
    split_view = teacher.reshape(token_rows, n_vocab, piece_cols)
    spread_view = lax.all_to_all(split_view, "vocab", split_axis=1, concat_axis=1, tiled=True)
    ordinal = jnp.arange(n_vocab, dtype=jnp.int32)
    matches = (shard_order[None, :] == ordinal[:, None]).astype(jnp.int32)
    inverse = jnp.sum(matches * ordinal[None, :], axis=1)
    sorted_view = jnp.take(spread_view, inverse, axis=1)
    return lax.all_to_all(sorted_view, "vocab", split_axis=1, concat_axis=1, tiled=True).reshape(
        token_rows, n_vocab * piece_cols
    )


def on_device(hidden, head, teacher, shard_order, loss_weight):
    n_dp, n_vocab = lax.axis_size("dp"), lax.axis_size("vocab")
    n_chips = n_vocab // 2
    tokens = hidden.shape[0] * n_dp

    if n_chips <= 4:
        other = xor_permute(teacher, "vocab", 1)
        plans = chip_plans(n_chips)
        number, flags = plan_chips(shard_order, plans, n_chips)
        chunks = [hidden] + [xor_permute(hidden, "dp", k) for k in range(1, n_dp)]

        def over_chips(x, pair):
            pairs = [(2 * z + c, 2 * pair[c][z] + c) for z in range(n_chips) for c in range(2)]
            return lax.ppermute(x, "vocab", pairs)

        arrived = lax.switch(
            number[0],
            [functools.partial(over_chips, pair=pair) for _, pair in plans],
            pick_call(flags, teacher, other),
        )
        chunks, arrived = lax.optimization_barrier((chunks, arrived))
        pieces = over_dp([arrived[k] for k in range(n_dp)])
        student, hid, stats = student_call(chunks, head, teacher, tokens)
        pieces, stats = lax.optimization_barrier((pieces, stats))
        mine = join_call(pieces)
        got = xor_permute(mine, "vocab", 1)
    else:
        chunks = [hidden] + [xor_permute(hidden, "dp", k) for k in range(1, n_dp)]
        student, hid, stats = student_call(chunks, head, teacher, tokens)
        block = wide_block(teacher, shard_order)
        cols, dp = block.shape[1] // n_dp, lax.axis_index("dp")
        mine = jnp.stack(
            over_dp([lax.dynamic_slice_in_dim(block, (dp ^ k) * cols, cols, 1) for k in range(n_dp)])
        )
        flags, got = jnp.ones((2,), jnp.int32), mine

    total_s, total_t = combine_stats(exchange(stats), tokens)
    parts = exchange(cross_call(flags, mine, got, student))
    logit_grad = logit_grad_call(flags, mine, got, student, total_s, total_t, loss_weight)
    head_grad = head_grad_call(logit_grad, hid)
    tops, terms = parts[:, 0, :tokens], parts[:, 0, tokens:]
    divergence = jnp.sum(terms * jnp.exp(tops - total_t), axis=0) - total_t + total_s
    return head_grad, divergence


def solution(mesh):
    in_specs = (P("dp", None), P("dp", "vocab", None), P("dp", "vocab"), P(), P())
    out_specs = (P("dp", "vocab", None), P())
    return jax.shard_map(
        on_device, mesh=mesh, in_specs=in_specs, out_specs=out_specs, check_vma=False
    )
```

```python
import functools
import itertools

import jax
import jax.numpy as jnp
import numpy as np
from jax import lax
from jax.experimental import pallas as pl
from jax.experimental.pallas import tpu as pltpu
from jax.sharding import PartitionSpec as P

MIB = 1024 * 1024
LOWEST = float(np.finfo(np.float32).min)
NO_PLAN = 2**30


def xor_permute(x, axis, k):
    size = lax.axis_size(axis)
    return lax.ppermute(x, axis, [(i, i ^ k) for i in range(size)])


def device_count():
    return lax.axis_size("dp") * lax.axis_size("vocab")


def exchange(copies):
    return lax.all_to_all(copies, ("dp", "vocab"), split_axis=0, concat_axis=0, tiled=True)


def log_sum_exp(parts, axis):
    top = jnp.max(parts, axis=axis, keepdims=True)
    total = jnp.sum(jnp.exp(parts - top), axis=axis, keepdims=True)
    return jnp.squeeze(top + jnp.log(total), axis)


def combine_stats(parts, tokens):
    n_dp, n_vocab = lax.axis_size("dp"), lax.axis_size("vocab")
    student = log_sum_exp(parts[:, 0, :tokens], 0)
    target = log_sum_exp(parts[:, 0, tokens:].reshape(n_dp, n_vocab, tokens // n_dp), 1)
    return student, target.reshape(tokens)


def place(rows):
    return lambda k: pl.multiple_of((lax.axis_index("dp") ^ k) * rows, rows)


def student_kernel(n_chunks, *refs):
    chunk_refs = refs[:n_chunks]
    head_ref, teacher_ref, out_ref, hid_out_ref, stats_ref = refs[n_chunks : n_chunks + 5]
    hid_ref, rows_ref, logits_ref, scores_ref, top_ref, sum_ref, stat_ref = refs[n_chunks + 5 : -4]
    chunk_sems, head_sems, out_sems, sems = refs[-4:]
    tokens, rows = scores_ref.shape
    own = teacher_ref.shape[0]
    block = min(256, rows)
    blocks = rows // block

    def head_copy(i):
        here = pl.ds(pl.multiple_of(i * block, block), block)
        return pltpu.make_async_copy(head_ref.at[0, here], rows_ref.at[here], head_sems.at[i])

    def out_copy(i):
        here = pl.ds(pl.multiple_of(i * block, block), block)
        return pltpu.make_async_copy(scores_ref.at[:, here], out_ref.at[:, here], out_sems.at[i])

    teacher_copy = pltpu.make_async_copy(teacher_ref, logits_ref, sems.at[0])
    hid_copy = pltpu.make_async_copy(hid_ref, hid_out_ref, sems.at[1])
    copies = []
    for k, ref in enumerate(chunk_refs):
        copies.append(
            pltpu.make_async_copy(ref, hid_ref.at[k * own : (k + 1) * own], chunk_sems.at[k])
        )
    teacher_copy.start()
    for copy in copies:
        copy.start()
    for i in range(blocks):
        head_copy(i).start()

    top_ref[...] = jnp.full(top_ref.shape, LOWEST, jnp.float32)
    sum_ref[...] = jnp.zeros(sum_ref.shape, jnp.float32)
    teacher_copy.wait()
    values = logits_ref[...].astype(jnp.float32)
    top = jnp.max(values, axis=1, keepdims=True)
    total = jnp.sum(jnp.exp(values - top), axis=1, keepdims=True)
    stat = jnp.transpose(jnp.broadcast_to(top + jnp.log(total), (own, 128)))[0:1]
    stats_ref[:, :, tokens:] = jnp.broadcast_to(stat[None], (stats_ref.shape[0], 1, own))
    for copy in copies:
        copy.wait()
    hid_copy.start()

    def scores_of(i):
        columns = pl.ds(pl.multiple_of(i * block, block), block)
        scores_ref[:, columns] = lax.dot_general(
            hid_ref[...], rows_ref[columns], (((1,), (1,)), ((), ())), preferred_element_type=jnp.float32
        )

    def stats_of(i):
        values = scores_ref[:, pl.ds(pl.multiple_of(i * block, block), block)]
        old = top_ref[...]
        top = jnp.maximum(old, jnp.max(values, axis=1, keepdims=True))
        total = jnp.sum(jnp.exp(values - top), axis=1, keepdims=True)
        top_ref[...] = top
        sum_ref[...] = sum_ref[...] * jnp.exp(old - top) + total

    def step(i, carry):
        head_copy(i).wait()
        stats_of(i - 1)
        scores_of(i)
        out_copy(i - 1).start()
        return carry

    head_copy(0).wait()
    scores_of(0)
    lax.fori_loop(1, blocks, step, 0)
    out_copy(blocks - 1).start()
    stats_of(blocks - 1)
    at = place(own)
    for k in range(n_chunks):
        here = slice(k * own, (k + 1) * own)
        stat = top_ref[here] + jnp.log(sum_ref[here])
        stat_ref[pl.ds(at(k), own)] = jnp.broadcast_to(stat, (own, 128))
    stat = jnp.transpose(stat_ref[...])[0:1]
    stats_ref[:, :, :tokens] = jnp.broadcast_to(stat[None], (stats_ref.shape[0], 1, tokens))
    for i in range(blocks):
        out_copy(i).wait()
    hid_copy.wait()


def student_call(chunks, head, teacher, tokens):
    _, rows, depth = head.shape
    blocks = rows // min(256, rows)
    in_hbm = pl.BlockSpec(memory_space=pltpu.HBM)
    return pl.pallas_call(
        functools.partial(student_kernel, len(chunks)),
        in_specs=[in_hbm] * (len(chunks) + 2),
        out_specs=[in_hbm, in_hbm, pl.BlockSpec(memory_space=pltpu.VMEM)],
        out_shape=[
            jax.ShapeDtypeStruct((tokens, rows), jnp.float32),
            jax.ShapeDtypeStruct((tokens, depth), jnp.bfloat16),
            jax.ShapeDtypeStruct((device_count(), 1, tokens + teacher.shape[0]), jnp.float32),
        ],
        scratch_shapes=[
            pltpu.VMEM((tokens, depth), jnp.bfloat16),
            pltpu.VMEM((rows, depth), jnp.bfloat16),
            pltpu.VMEM(teacher.shape, jnp.bfloat16),
            pltpu.VMEM((tokens, rows), jnp.float32),
            pltpu.VMEM((tokens, 1), jnp.float32),
            pltpu.VMEM((tokens, 1), jnp.float32),
            pltpu.VMEM((tokens, 128), jnp.float32),
            pltpu.SemaphoreType.DMA((len(chunks),)),
            pltpu.SemaphoreType.DMA((blocks,)),
            pltpu.SemaphoreType.DMA((blocks,)),
            pltpu.SemaphoreType.DMA((2,)),
        ],
        compiler_params=pltpu.CompilerParams(vmem_limit_bytes=60 * MIB),
        cost_estimate=pl.CostEstimate(
            flops=2 * tokens * rows * depth,
            bytes_accessed=2 * rows * depth + 2 * tokens * depth + 4 * tokens * rows,
            transcendentals=tokens * rows,
        ),
        name="student",
    )(*chunks, head, teacher)


def cross_kernel(flags_ref, mine_ref, got_ref, scores_ref, out_ref, col_ref):
    step, last = pl.program_id(0), pl.num_programs(0) - 1
    rows = scores_ref.shape[0]
    tokens = col_ref.shape[0]
    half = rows // 2
    at = place(rows)(step)
    keep = flags_ref[1] != 0
    lane = lax.broadcasted_iota(jnp.int32, (half, 128), 1)
    for first in (0, half):
        part = slice(first, first + half)
        here = pl.ds(pl.multiple_of(at + first, half), half)
        target = jnp.where(keep, mine_ref[0, part], got_ref[0, part]).astype(jnp.float32)
        top = jnp.max(target, axis=1, keepdims=True)
        cross = jnp.exp(target - top) * (target - scores_ref[part])
        col_ref[here] = jnp.where(lane == 0, top, jnp.sum(cross, axis=1, keepdims=True))

    @pl.when(step == last)
    def _():
        lines = jnp.transpose(col_ref[...])
        for i in range(2):
            line = jnp.broadcast_to(lines[i : i + 1][None], (out_ref.shape[0], 1, tokens))
            out_ref[:, :, i * tokens : (i + 1) * tokens] = line


def block_specs(n_dp, part, rows):
    return [
        pl.BlockSpec(memory_space=pltpu.SMEM),
        pl.BlockSpec((1, part, rows), lambda k: (k, 0, 0)),
        pl.BlockSpec((1, part, rows), lambda k: (k, 0, 0)),
        pl.BlockSpec((part, rows), lambda k: (k, 0)),
    ]


def cross_call(flags, mine, got, scores):
    n_dp, part, rows = mine.shape
    tokens = n_dp * part
    shape = (device_count(), 1, 2 * tokens)
    return pl.pallas_call(
        cross_kernel,
        grid=(n_dp,),
        in_specs=block_specs(n_dp, part, rows),
        out_specs=pl.BlockSpec(shape, lambda k: (0, 0, 0)),
        out_shape=jax.ShapeDtypeStruct(shape, jnp.float32),
        scratch_shapes=[pltpu.VMEM((tokens, 128), jnp.float32)],
        compiler_params=pltpu.CompilerParams(vmem_limit_bytes=24 * MIB),
        cost_estimate=pl.CostEstimate(
            flops=5 * tokens * rows, bytes_accessed=8 * tokens * rows, transcendentals=tokens * rows
        ),
        name="cross",
    )(flags, mine, got, scores)


def head_grad_kernel(
    flags_ref, mine_ref, got_ref, scores_in_ref, hid_in_ref, row_s_ref, row_t_ref, weight_ref, out_ref,
    target_ref, scores_ref, hid_ref, grad_ref, col_ref, target_sems, scores_sems, hid_sem,
):
    n_dp, rows, _ = target_ref.shape
    tokens = n_dp * rows
    block = out_ref.shape[1]
    step = pl.program_id(0)

    @pl.when(step == 0)
    def _():
        at = place(rows)
        half = rows // 2
        hid_copy = pltpu.make_async_copy(hid_in_ref, hid_ref, hid_sem)

        def target_copy(ref, k):
            return pltpu.make_async_copy(ref.at[k], target_ref.at[k], target_sems.at[k])

        def scores_copy(k):
            here = pl.ds(pl.multiple_of(k * rows, rows), rows)
            return pltpu.make_async_copy(
                scores_in_ref.at[here], scores_ref.at[here], scores_sems.at[k]
            )

        for k in range(n_dp):
            scores_copy(k).start()

            @pl.when(flags_ref[1] != 0)
            def _():
                target_copy(mine_ref, k).start()

            @pl.when(flags_ref[1] == 0)
            def _():
                target_copy(got_ref, k).start()

        hid_copy.start()
        line = lax.broadcasted_iota(jnp.int32, (128, tokens), 0)
        col_ref[...] = jnp.transpose(
            jnp.where(line == 0, row_s_ref[...], jnp.where(line == 1, row_t_ref[...], weight_ref[...]))
        )

        def piece(k, carry):
            scores_copy(k).wait()
            target_copy(mine_ref, k).wait()
            for first in (0, half):
                part = pl.ds(pl.multiple_of(k * rows + first, half), half)
                cols = col_ref[pl.ds(pl.multiple_of(at(k) + first, half), half)]
                target = target_ref[k, first : first + half].astype(jnp.float32)
                prob_s = jnp.exp(scores_ref[part] - cols[:, 0:1])
                prob_t = jnp.exp(target - cols[:, 1:2])
                grad_ref[part] = (cols[:, 2:3] * (prob_s - prob_t)).astype(jnp.bfloat16)
            return carry

        lax.fori_loop(0, n_dp, piece, 0)
        hid_copy.wait()

    ids = pl.ds(pl.multiple_of(step * block, block), block)
    out_ref[0] = lax.dot_general(
        grad_ref[:, ids], hid_ref[...], (((0,), (0,)), ((), ())), preferred_element_type=jnp.float32
    ).astype(jnp.bfloat16)


def head_grad_call(flags, mine, got, scores, hid, total_s, total_t, weight):
    n_dp, part, rows = mine.shape
    tokens, depth = hid.shape
    block = min(256, rows)
    in_hbm = pl.BlockSpec(memory_space=pltpu.HBM)
    whole_row = pl.BlockSpec((1, tokens), lambda i: (0, 0))
    return pl.pallas_call(
        head_grad_kernel,
        grid=(rows // block,),
        in_specs=[pl.BlockSpec(memory_space=pltpu.SMEM)] + [in_hbm] * 4 + [whole_row] * 3,
        out_specs=pl.BlockSpec((1, block, depth), lambda i: (0, i, 0)),
        out_shape=jax.ShapeDtypeStruct((1, rows, depth), jnp.bfloat16),
        scratch_shapes=[
            pltpu.VMEM(mine.shape, jnp.bfloat16),
            pltpu.VMEM((tokens, rows), jnp.float32),
            pltpu.VMEM((tokens, depth), jnp.bfloat16),
            pltpu.VMEM((tokens, rows), jnp.bfloat16),
            pltpu.VMEM((tokens, 128), jnp.float32),
            pltpu.SemaphoreType.DMA((n_dp,)),
            pltpu.SemaphoreType.DMA((n_dp,)),
            pltpu.SemaphoreType.DMA,
        ],
        compiler_params=pltpu.CompilerParams(vmem_limit_bytes=60 * MIB),
        cost_estimate=pl.CostEstimate(
            flops=2 * tokens * rows * depth,
            bytes_accessed=2 * rows * depth + 2 * tokens * depth + 6 * tokens * rows,
            transcendentals=2 * tokens * rows,
        ),
        name="head_grad",
    )(flags, mine, got, scores, hid, total_s[None], total_t[None], weight[None])


def chip_plans(n):
    def load(pair):
        ups = [sum(z < c <= p[z] for p in pair for z in range(n)) for c in range(1, n)]
        return max(ups), sum(ups)

    best = {}
    perms = list(itertools.permutations(range(n)))
    for pair in itertools.combinations_with_replacement(perms, 2):
        code = sum(3 ** (n * z + p[z]) for p in pair for z in range(n))
        if code not in best or load(pair) < load(best[code]):
            best[code] = pair
    return sorted(best.items())


def plan_tables(plans, n):
    codes = [code for code, _ in plans]
    keys = [
        (i << 8) | sum(first[z] << (2 * z) for z in range(n)) for i, (_, (first, _)) in enumerate(plans)
    ]
    pad = -len(codes) % 1024
    codes = np.array(codes + [-1] * pad, np.int32).reshape(-1, 128)
    keys = np.array(keys + [NO_PLAN] * pad, np.int32).reshape(-1, 128)
    return codes, keys


def plan_kernel(n_chips, order_ref, codes_ref, keys_ref, number_ref, flags_ref):
    chip = lax.axis_index("vocab") // 2
    code = jnp.int32(0)
    for block in range(2 * n_chips):
        dest = order_ref[block] // 2
        power = jnp.int32(0)
        for d in range(n_chips):
            power = jnp.where(dest == d, 3 ** (n_chips * (block // 2) + d), power)
        code = code + power
    key = jnp.min(jnp.where(codes_ref[...] == code, keys_ref[...], NO_PLAN))
    sends = jnp.int32(0)
    arrives = jnp.int32(0)
    for z in range(n_chips):
        goes = (key >> (2 * z)) & 3
        source = jnp.where(order_ref[2 * z] // 2 == goes, 0, 1)
        meant = jnp.where(source == 0, order_ref[2 * z], order_ref[2 * z + 1]) & 1
        sends = jnp.where(chip == z, source, sends)
        arrives = jnp.where(goes == chip, meant, arrives)
    number_ref[0] = key >> 8
    flags_ref[0] = 1 - sends
    flags_ref[1] = 1 - arrives


def plan_chips(shard_order, plans, n_chips):
    codes, keys = plan_tables(plans, n_chips)
    in_smem = pl.BlockSpec(memory_space=pltpu.SMEM)
    in_vmem = pl.BlockSpec(memory_space=pltpu.VMEM)
    return pl.pallas_call(
        functools.partial(plan_kernel, n_chips),
        in_specs=[in_smem, in_vmem, in_vmem],
        out_specs=[in_smem] * 2,
        out_shape=[jax.ShapeDtypeStruct((n,), jnp.int32) for n in (1, 2)],
        compiler_params=pltpu.CompilerParams(vmem_limit_bytes=60 * MIB),
        name="plan",
    )(shard_order, jnp.asarray(codes), jnp.asarray(keys))


def pick_kernel(flags_ref, mine_ref, other_ref, out_ref):
    dp = lax.axis_index("dp")
    n_dp, _, cols = out_ref.shape
    own = flags_ref[0] != 0
    for k in range(n_dp):
        here = pl.ds(pl.multiple_of((dp ^ k) * cols, cols), cols)
        out_ref[k] = jnp.where(own, mine_ref[:, here], other_ref[:, here])


def pick_call(flags, mine, other):
    n_dp = lax.axis_size("dp")
    shape = (n_dp, mine.shape[0], mine.shape[1] // n_dp)
    in_vmem = pl.BlockSpec(memory_space=pltpu.VMEM)
    return pl.pallas_call(
        pick_kernel,
        in_specs=[pl.BlockSpec(memory_space=pltpu.SMEM), in_vmem, in_vmem],
        out_specs=in_vmem,
        out_shape=jax.ShapeDtypeStruct(shape, jnp.bfloat16),
        compiler_params=pltpu.CompilerParams(vmem_limit_bytes=24 * MIB),
        name="pick",
    )(flags, mine, other)


def join_kernel(*refs):
    for k, ref in enumerate(refs[:-1]):
        refs[-1][k] = ref[...]


def join_call(pieces):
    in_vmem = pl.BlockSpec(memory_space=pltpu.VMEM)
    return pl.pallas_call(
        join_kernel,
        in_specs=[in_vmem] * len(pieces),
        out_specs=in_vmem,
        out_shape=jax.ShapeDtypeStruct((len(pieces), *pieces[0].shape), jnp.bfloat16),
        compiler_params=pltpu.CompilerParams(vmem_limit_bytes=24 * MIB),
        name="join",
    )(*pieces)


def over_dp(pieces):
    return [pieces[0]] + [xor_permute(pieces[k], "dp", k) for k in range(1, len(pieces))]


def wide_block(teacher, shard_order):
    token_rows = teacher.shape[0]
    n_vocab = lax.axis_size("vocab")
    piece_cols = teacher.shape[1] // n_vocab
    split_view = teacher.reshape(token_rows, n_vocab, piece_cols)
    spread_view = lax.all_to_all(split_view, "vocab", split_axis=1, concat_axis=1, tiled=True)
    ordinal = jnp.arange(n_vocab, dtype=jnp.int32)
    matches = (shard_order[None, :] == ordinal[:, None]).astype(jnp.int32)
    inverse = jnp.sum(matches * ordinal[None, :], axis=1)
    sorted_view = jnp.take(spread_view, inverse, axis=1)
    return lax.all_to_all(sorted_view, "vocab", split_axis=1, concat_axis=1, tiled=True).reshape(
        token_rows, n_vocab * piece_cols
    )


def on_device(hidden, head, teacher, shard_order, loss_weight):
    n_dp, n_vocab = lax.axis_size("dp"), lax.axis_size("vocab")
    n_chips = n_vocab // 2
    tokens = hidden.shape[0] * n_dp

    if n_chips <= 4:
        other = xor_permute(teacher, "vocab", 1)
        plans = chip_plans(n_chips)
        number, flags = plan_chips(shard_order, plans, n_chips)
        chunks = [hidden] + [xor_permute(hidden, "dp", k) for k in range(1, n_dp)]

        def over_chips(x, pair):
            pairs = [(2 * z + c, 2 * pair[c][z] + c) for z in range(n_chips) for c in range(2)]
            return lax.ppermute(x, "vocab", pairs)

        arrived = lax.switch(
            number[0],
            [functools.partial(over_chips, pair=pair) for _, pair in plans],
            pick_call(flags, teacher, other),
        )
        chunks, arrived = lax.optimization_barrier((chunks, arrived))
        pieces = over_dp([arrived[k] for k in range(n_dp)])
        student, hid, stats = student_call(chunks, head, teacher, tokens)
        pieces, stats = lax.optimization_barrier((pieces, stats))
        mine = join_call(pieces)
        got = xor_permute(mine, "vocab", 1)
    else:
        chunks = [hidden] + [xor_permute(hidden, "dp", k) for k in range(1, n_dp)]
        student, hid, stats = student_call(chunks, head, teacher, tokens)
        block = wide_block(teacher, shard_order)
        cols, dp = block.shape[1] // n_dp, lax.axis_index("dp")
        mine = jnp.stack(
            over_dp([lax.dynamic_slice_in_dim(block, (dp ^ k) * cols, cols, 1) for k in range(n_dp)])
        )
        flags, got = jnp.ones((2,), jnp.int32), mine

    sent = cross_call(flags, mine, got, student)
    parts, sent = lax.optimization_barrier((exchange(stats), sent))
    total_s, total_t = combine_stats(parts, tokens)
    head_grad = head_grad_call(flags, mine, got, student, hid, total_s, total_t, loss_weight)
    parts, head_grad = lax.optimization_barrier((exchange(sent), head_grad))
    tops, terms = parts[:, 0, :tokens], parts[:, 0, tokens:]
    divergence = jnp.sum(terms * jnp.exp(tops - total_t), axis=0) - total_t + total_s
    return head_grad, divergence


def solution(mesh):
    in_specs = (P("dp", None), P("dp", "vocab", None), P("dp", "vocab"), P(), P())
    out_specs = (P("dp", "vocab", None), P())
    return jax.shard_map(
        on_device, mesh=mesh, in_specs=in_specs, out_specs=out_specs, check_vma=False
    )
```

```python
import functools
import itertools

import jax
import jax.numpy as jnp
import numpy as np
from jax import lax
from jax.experimental import pallas as pl
from jax.experimental.pallas import tpu as pltpu
from jax.sharding import PartitionSpec as P

MIB = 1024 * 1024
LOWEST = float(np.finfo(np.float32).min)
NO_PLAN = 2**30


def xor_permute(x, axis, k):
    size = lax.axis_size(axis)
    return lax.ppermute(x, axis, [(i, i ^ k) for i in range(size)])


def device_count():
    return lax.axis_size("dp") * lax.axis_size("vocab")


def exchange(copies):
    return lax.all_to_all(copies, ("dp", "vocab"), split_axis=0, concat_axis=0, tiled=True)


def log_sum_exp(values):
    top = jnp.max(values, axis=0, keepdims=True)
    return top + jnp.log(jnp.sum(jnp.exp(values - top), axis=0, keepdims=True))


def place(rows):
    return lambda k: pl.multiple_of((lax.axis_index("dp") ^ k) * rows, rows)


def student_kernel(n_chunks, *refs):
    chunk_refs = refs[:n_chunks]
    head_ref, teacher_ref, out_ref, hid_out_ref, stats_ref = refs[n_chunks : n_chunks + 5]
    hid_ref, rows_ref, logits_ref, scores_ref, top_ref, sum_ref, stat_ref = refs[n_chunks + 5 : -4]
    chunk_sems, head_sems, out_sems, sems = refs[-4:]
    tokens, rows = scores_ref.shape
    own = teacher_ref.shape[0]
    block = min(256, rows)
    blocks = rows // block

    def head_copy(i):
        here = pl.ds(pl.multiple_of(i * block, block), block)
        return pltpu.make_async_copy(head_ref.at[0, here], rows_ref.at[here], head_sems.at[i])

    def out_copy(i):
        here = pl.ds(pl.multiple_of(i * block, block), block)
        return pltpu.make_async_copy(scores_ref.at[:, here], out_ref.at[:, here], out_sems.at[i])

    teacher_copy = pltpu.make_async_copy(teacher_ref, logits_ref, sems.at[0])
    hid_copy = pltpu.make_async_copy(hid_ref, hid_out_ref, sems.at[1])
    copies = []
    for k, ref in enumerate(chunk_refs):
        copies.append(
            pltpu.make_async_copy(ref, hid_ref.at[k * own : (k + 1) * own], chunk_sems.at[k])
        )
    teacher_copy.start()
    for copy in copies:
        copy.start()
    for i in range(blocks):
        head_copy(i).start()

    top_ref[...] = jnp.full(top_ref.shape, LOWEST, jnp.float32)
    sum_ref[...] = jnp.zeros(sum_ref.shape, jnp.float32)
    teacher_copy.wait()
    values = logits_ref[...].astype(jnp.float32)
    top = jnp.max(values, axis=1, keepdims=True)
    total = jnp.sum(jnp.exp(values - top), axis=1, keepdims=True)
    stat = jnp.transpose(jnp.broadcast_to(top + jnp.log(total), (own, 128)))[0:1]
    stats_ref[:, :, tokens:] = jnp.broadcast_to(stat[None], (stats_ref.shape[0], 1, own))
    for copy in copies:
        copy.wait()
    hid_copy.start()

    def scores_of(i):
        columns = pl.ds(pl.multiple_of(i * block, block), block)
        scores_ref[:, columns] = lax.dot_general(
            hid_ref[...], rows_ref[columns], (((1,), (1,)), ((), ())), preferred_element_type=jnp.float32
        )

    def stats_of(i):
        values = scores_ref[:, pl.ds(pl.multiple_of(i * block, block), block)]
        old = top_ref[...]
        top = jnp.maximum(old, jnp.max(values, axis=1, keepdims=True))
        total = jnp.sum(jnp.exp(values - top), axis=1, keepdims=True)
        top_ref[...] = top
        sum_ref[...] = sum_ref[...] * jnp.exp(old - top) + total

    def step(i, carry):
        head_copy(i).wait()
        stats_of(i - 1)
        scores_of(i)
        out_copy(i - 1).start()
        return carry

    head_copy(0).wait()
    scores_of(0)
    lax.fori_loop(1, blocks, step, 0)
    out_copy(blocks - 1).start()
    stats_of(blocks - 1)
    at = place(own)
    for k in range(n_chunks):
        here = slice(k * own, (k + 1) * own)
        stat = top_ref[here] + jnp.log(sum_ref[here])
        stat_ref[pl.ds(at(k), own)] = jnp.broadcast_to(stat, (own, 128))
    stat = jnp.transpose(stat_ref[...])[0:1]
    stats_ref[:, :, :tokens] = jnp.broadcast_to(stat[None], (stats_ref.shape[0], 1, tokens))
    for i in range(blocks):
        out_copy(i).wait()
    hid_copy.wait()


def student_call(chunks, head, teacher, tokens):
    _, rows, depth = head.shape
    blocks = rows // min(256, rows)
    in_hbm = pl.BlockSpec(memory_space=pltpu.HBM)
    return pl.pallas_call(
        functools.partial(student_kernel, len(chunks)),
        in_specs=[in_hbm] * (len(chunks) + 2),
        out_specs=[in_hbm, in_hbm, pl.BlockSpec(memory_space=pltpu.VMEM)],
        out_shape=[
            jax.ShapeDtypeStruct((tokens, rows), jnp.float32),
            jax.ShapeDtypeStruct((tokens, depth), jnp.bfloat16),
            jax.ShapeDtypeStruct((device_count(), 1, tokens + teacher.shape[0]), jnp.float32),
        ],
        scratch_shapes=[
            pltpu.VMEM((tokens, depth), jnp.bfloat16),
            pltpu.VMEM((rows, depth), jnp.bfloat16),
            pltpu.VMEM(teacher.shape, jnp.bfloat16),
            pltpu.VMEM((tokens, rows), jnp.float32),
            pltpu.VMEM((tokens, 1), jnp.float32),
            pltpu.VMEM((tokens, 1), jnp.float32),
            pltpu.VMEM((tokens, 128), jnp.float32),
            pltpu.SemaphoreType.DMA((len(chunks),)),
            pltpu.SemaphoreType.DMA((blocks,)),
            pltpu.SemaphoreType.DMA((blocks,)),
            pltpu.SemaphoreType.DMA((2,)),
        ],
        compiler_params=pltpu.CompilerParams(vmem_limit_bytes=60 * MIB),
        cost_estimate=pl.CostEstimate(
            flops=2 * tokens * rows * depth,
            bytes_accessed=2 * rows * depth + 2 * tokens * depth + 4 * tokens * rows,
            transcendentals=tokens * rows,
        ),
        name="student",
    )(*chunks, head, teacher)


def cross_kernel(flags_ref, mine_ref, got_ref, scores_ref, out_ref, col_ref):
    step, last = pl.program_id(0), pl.num_programs(0) - 1
    rows = scores_ref.shape[0]
    tokens = col_ref.shape[0]
    half = rows // 2
    at = place(rows)(step)
    keep = flags_ref[1] != 0
    lane = lax.broadcasted_iota(jnp.int32, (half, 128), 1)
    for first in (0, half):
        part = slice(first, first + half)
        here = pl.ds(pl.multiple_of(at + first, half), half)
        target = jnp.where(keep, mine_ref[0, part], got_ref[0, part]).astype(jnp.float32)
        top = jnp.max(target, axis=1, keepdims=True)
        cross = jnp.exp(target - top) * (target - scores_ref[part])
        col_ref[here] = jnp.where(lane == 0, top, jnp.sum(cross, axis=1, keepdims=True))

    @pl.when(step == last)
    def _():
        lines = jnp.transpose(col_ref[...])
        for i in range(2):
            line = jnp.broadcast_to(lines[i : i + 1][None], (out_ref.shape[0], 1, tokens))
            out_ref[:, :, i * tokens : (i + 1) * tokens] = line


def block_specs(n_dp, part, rows):
    return [
        pl.BlockSpec(memory_space=pltpu.SMEM),
        pl.BlockSpec((1, part, rows), lambda k: (k, 0, 0)),
        pl.BlockSpec((1, part, rows), lambda k: (k, 0, 0)),
        pl.BlockSpec((part, rows), lambda k: (k, 0)),
    ]


def cross_call(flags, mine, got, scores):
    n_dp, part, rows = mine.shape
    tokens = n_dp * part
    shape = (device_count(), 1, 2 * tokens)
    return pl.pallas_call(
        cross_kernel,
        grid=(n_dp,),
        in_specs=block_specs(n_dp, part, rows),
        out_specs=pl.BlockSpec(shape, lambda k: (0, 0, 0)),
        out_shape=jax.ShapeDtypeStruct(shape, jnp.float32),
        scratch_shapes=[pltpu.VMEM((tokens, 128), jnp.float32)],
        compiler_params=pltpu.CompilerParams(vmem_limit_bytes=24 * MIB),
        cost_estimate=pl.CostEstimate(
            flops=5 * tokens * rows, bytes_accessed=8 * tokens * rows, transcendentals=tokens * rows
        ),
        name="cross",
    )(flags, mine, got, scores)


def head_grad_kernel(
    flags_ref, mine_ref, got_ref, scores_in_ref, hid_in_ref, stats_ref, weight_ref, out_ref, totals_ref,
    target_ref, scores_ref, hid_ref, grad_ref, col_ref, target_sems, scores_sems, hid_sem,
):
    n_dp, rows, _ = target_ref.shape
    tokens = n_dp * rows
    block = out_ref.shape[1]
    step = pl.program_id(0)

    @pl.when(step == 0)
    def _():
        at = place(rows)
        half = rows // 2
        hid_copy = pltpu.make_async_copy(hid_in_ref, hid_ref, hid_sem)

        def target_copy(ref, k):
            return pltpu.make_async_copy(ref.at[k], target_ref.at[k], target_sems.at[k])

        def scores_copy(k):
            here = pl.ds(pl.multiple_of(k * rows, rows), rows)
            return pltpu.make_async_copy(
                scores_in_ref.at[here], scores_ref.at[here], scores_sems.at[k]
            )

        for k in range(n_dp):
            scores_copy(k).start()

            @pl.when(flags_ref[1] != 0)
            def _():
                target_copy(mine_ref, k).start()

            @pl.when(flags_ref[1] == 0)
            def _():
                target_copy(got_ref, k).start()

        hid_copy.start()
        n_vocab = stats_ref.shape[0] // n_dp
        total_s = log_sum_exp(stats_ref[:, 0, :tokens])
        total_t = jnp.concatenate(
            [
                log_sum_exp(stats_ref[d * n_vocab : (d + 1) * n_vocab, 0, tokens:])
                for d in range(n_dp)
            ],
            axis=1,
        )
        totals_ref[0:1] = total_s
        totals_ref[1:2] = total_t
        line = lax.broadcasted_iota(jnp.int32, (128, tokens), 0)
        col_ref[...] = jnp.transpose(
            jnp.where(line == 0, total_s, jnp.where(line == 1, total_t, weight_ref[...]))
        )

        def piece(k, carry):
            scores_copy(k).wait()
            target_copy(mine_ref, k).wait()
            for first in (0, half):
                part = pl.ds(pl.multiple_of(k * rows + first, half), half)
                cols = col_ref[pl.ds(pl.multiple_of(at(k) + first, half), half)]
                target = target_ref[k, first : first + half].astype(jnp.float32)
                prob_s = jnp.exp(scores_ref[part] - cols[:, 0:1])
                prob_t = jnp.exp(target - cols[:, 1:2])
                grad_ref[part] = (cols[:, 2:3] * (prob_s - prob_t)).astype(jnp.bfloat16)
            return carry

        lax.fori_loop(0, n_dp, piece, 0)
        hid_copy.wait()

    ids = pl.ds(pl.multiple_of(step * block, block), block)
    out_ref[0] = lax.dot_general(
        grad_ref[:, ids], hid_ref[...], (((0,), (0,)), ((), ())), preferred_element_type=jnp.float32
    ).astype(jnp.bfloat16)


def head_grad_call(flags, mine, got, scores, hid, stats, weight):
    n_dp, part, rows = mine.shape
    tokens, depth = hid.shape
    block = min(256, rows)
    in_hbm = pl.BlockSpec(memory_space=pltpu.HBM)
    return pl.pallas_call(
        head_grad_kernel,
        grid=(rows // block,),
        in_specs=[pl.BlockSpec(memory_space=pltpu.SMEM)] + [in_hbm] * 4
        + [pl.BlockSpec(stats.shape, lambda i: (0, 0, 0)), pl.BlockSpec((1, tokens), lambda i: (0, 0))],
        out_specs=[
            pl.BlockSpec((1, block, depth), lambda i: (0, i, 0)),
            pl.BlockSpec((2, tokens), lambda i: (0, 0)),
        ],
        out_shape=[
            jax.ShapeDtypeStruct((1, rows, depth), jnp.bfloat16),
            jax.ShapeDtypeStruct((2, tokens), jnp.float32),
        ],
        scratch_shapes=[
            pltpu.VMEM(mine.shape, jnp.bfloat16),
            pltpu.VMEM((tokens, rows), jnp.float32),
            pltpu.VMEM((tokens, depth), jnp.bfloat16),
            pltpu.VMEM((tokens, rows), jnp.bfloat16),
            pltpu.VMEM((tokens, 128), jnp.float32),
            pltpu.SemaphoreType.DMA((n_dp,)),
            pltpu.SemaphoreType.DMA((n_dp,)),
            pltpu.SemaphoreType.DMA,
        ],
        compiler_params=pltpu.CompilerParams(vmem_limit_bytes=60 * MIB),
        cost_estimate=pl.CostEstimate(
            flops=2 * tokens * rows * depth,
            bytes_accessed=2 * rows * depth + 2 * tokens * depth + 6 * tokens * rows,
            transcendentals=2 * tokens * rows,
        ),
        name="head_grad",
    )(flags, mine, got, scores, hid, stats, weight[None])


def chip_plans(n):
    def load(pair):
        ups = [sum(z < c <= p[z] for p in pair for z in range(n)) for c in range(1, n)]
        return max(ups), sum(ups)

    best = {}
    perms = list(itertools.permutations(range(n)))
    for pair in itertools.combinations_with_replacement(perms, 2):
        code = sum(3 ** (n * z + p[z]) for p in pair for z in range(n))
        if code not in best or load(pair) < load(best[code]):
            best[code] = pair
    return sorted(best.items())


def plan_tables(plans, n):
    codes = [code for code, _ in plans]
    keys = [
        (i << 8) | sum(first[z] << (2 * z) for z in range(n)) for i, (_, (first, _)) in enumerate(plans)
    ]
    pad = -len(codes) % 1024
    codes = np.array(codes + [-1] * pad, np.int32).reshape(-1, 128)
    keys = np.array(keys + [NO_PLAN] * pad, np.int32).reshape(-1, 128)
    return codes, keys


def plan_kernel(n_chips, order_ref, codes_ref, keys_ref, number_ref, flags_ref):
    chip = lax.axis_index("vocab") // 2
    code = jnp.int32(0)
    for block in range(2 * n_chips):
        dest = order_ref[block] // 2
        power = jnp.int32(0)
        for d in range(n_chips):
            power = jnp.where(dest == d, 3 ** (n_chips * (block // 2) + d), power)
        code = code + power
    key = jnp.min(jnp.where(codes_ref[...] == code, keys_ref[...], NO_PLAN))
    sends = jnp.int32(0)
    arrives = jnp.int32(0)
    for z in range(n_chips):
        goes = (key >> (2 * z)) & 3
        source = jnp.where(order_ref[2 * z] // 2 == goes, 0, 1)
        meant = jnp.where(source == 0, order_ref[2 * z], order_ref[2 * z + 1]) & 1
        sends = jnp.where(chip == z, source, sends)
        arrives = jnp.where(goes == chip, meant, arrives)
    number_ref[0] = key >> 8
    flags_ref[0] = 1 - sends
    flags_ref[1] = 1 - arrives


def plan_chips(shard_order, plans, n_chips):
    codes, keys = plan_tables(plans, n_chips)
    in_smem = pl.BlockSpec(memory_space=pltpu.SMEM)
    in_vmem = pl.BlockSpec(memory_space=pltpu.VMEM)
    return pl.pallas_call(
        functools.partial(plan_kernel, n_chips),
        in_specs=[in_smem, in_vmem, in_vmem],
        out_specs=[in_smem] * 2,
        out_shape=[jax.ShapeDtypeStruct((n,), jnp.int32) for n in (1, 2)],
        compiler_params=pltpu.CompilerParams(vmem_limit_bytes=60 * MIB),
        name="plan",
    )(shard_order, jnp.asarray(codes), jnp.asarray(keys))


def pick_kernel(flags_ref, mine_ref, other_ref, out_ref):
    dp = lax.axis_index("dp")
    n_dp, _, cols = out_ref.shape
    own = flags_ref[0] != 0
    for k in range(n_dp):
        here = pl.ds(pl.multiple_of((dp ^ k) * cols, cols), cols)
        out_ref[k] = jnp.where(own, mine_ref[:, here], other_ref[:, here])


def pick_call(flags, mine, other):
    n_dp = lax.axis_size("dp")
    shape = (n_dp, mine.shape[0], mine.shape[1] // n_dp)
    in_vmem = pl.BlockSpec(memory_space=pltpu.VMEM)
    return pl.pallas_call(
        pick_kernel,
        in_specs=[pl.BlockSpec(memory_space=pltpu.SMEM), in_vmem, in_vmem],
        out_specs=in_vmem,
        out_shape=jax.ShapeDtypeStruct(shape, jnp.bfloat16),
        compiler_params=pltpu.CompilerParams(vmem_limit_bytes=24 * MIB),
        name="pick",
    )(flags, mine, other)


def join_kernel(*refs):
    for k, ref in enumerate(refs[:-1]):
        refs[-1][k] = ref[...]


def join_call(pieces):
    in_vmem = pl.BlockSpec(memory_space=pltpu.VMEM)
    return pl.pallas_call(
        join_kernel,
        in_specs=[in_vmem] * len(pieces),
        out_specs=in_vmem,
        out_shape=jax.ShapeDtypeStruct((len(pieces), *pieces[0].shape), jnp.bfloat16),
        compiler_params=pltpu.CompilerParams(vmem_limit_bytes=24 * MIB),
        name="join",
    )(*pieces)


def over_dp(pieces):
    return [pieces[0]] + [xor_permute(pieces[k], "dp", k) for k in range(1, len(pieces))]


def wide_block(teacher, shard_order):
    token_rows = teacher.shape[0]
    n_vocab = lax.axis_size("vocab")
    piece_cols = teacher.shape[1] // n_vocab
    split_view = teacher.reshape(token_rows, n_vocab, piece_cols)
    spread_view = lax.all_to_all(split_view, "vocab", split_axis=1, concat_axis=1, tiled=True)
    ordinal = jnp.arange(n_vocab, dtype=jnp.int32)
    matches = (shard_order[None, :] == ordinal[:, None]).astype(jnp.int32)
    inverse = jnp.sum(matches * ordinal[None, :], axis=1)
    sorted_view = jnp.take(spread_view, inverse, axis=1)
    return lax.all_to_all(sorted_view, "vocab", split_axis=1, concat_axis=1, tiled=True).reshape(
        token_rows, n_vocab * piece_cols
    )


def on_device(hidden, head, teacher, shard_order, loss_weight):
    n_dp, n_vocab = lax.axis_size("dp"), lax.axis_size("vocab")
    n_chips = n_vocab // 2
    tokens = hidden.shape[0] * n_dp

    if n_chips <= 4:
        other = xor_permute(teacher, "vocab", 1)
        plans = chip_plans(n_chips)
        number, flags = plan_chips(shard_order, plans, n_chips)
        chunks = [hidden] + [xor_permute(hidden, "dp", k) for k in range(1, n_dp)]

        def over_chips(x, pair):
            pairs = [(2 * z + c, 2 * pair[c][z] + c) for z in range(n_chips) for c in range(2)]
            return lax.ppermute(x, "vocab", pairs)

        arrived = lax.switch(
            number[0],
            [functools.partial(over_chips, pair=pair) for _, pair in plans],
            pick_call(flags, teacher, other),
        )
        chunks, arrived = lax.optimization_barrier((chunks, arrived))
        pieces = over_dp([arrived[k] for k in range(n_dp)])
        student, hid, stats = student_call(chunks, head, teacher, tokens)
        pieces, _ = lax.optimization_barrier((pieces, stats))
        mine = join_call(pieces)
        got = xor_permute(mine, "vocab", 1)
    else:
        chunks = [hidden] + [xor_permute(hidden, "dp", k) for k in range(1, n_dp)]
        student, hid, stats = student_call(chunks, head, teacher, tokens)
        block = wide_block(teacher, shard_order)
        cols, dp = block.shape[1] // n_dp, lax.axis_index("dp")
        mine = jnp.stack(
            over_dp([lax.dynamic_slice_in_dim(block, (dp ^ k) * cols, cols, 1) for k in range(n_dp)])
        )
        flags, got = jnp.ones((2,), jnp.int32), mine

    sent = cross_call(flags, mine, got, student)
    parts, sent = lax.optimization_barrier((exchange(stats), sent))
    head_grad, totals = head_grad_call(flags, mine, got, student, hid, parts, loss_weight)
    parts, head_grad = lax.optimization_barrier((exchange(sent), head_grad))
    total_s, total_t = totals[0], totals[1]
    tops, terms = parts[:, 0, :tokens], parts[:, 0, tokens:]
    divergence = jnp.sum(terms * jnp.exp(tops - total_t), axis=0) - total_t + total_s
    return head_grad, divergence


def solution(mesh):
    in_specs = (P("dp", None), P("dp", "vocab", None), P("dp", "vocab"), P(), P())
    out_specs = (P("dp", "vocab", None), P())
    return jax.shard_map(
        on_device, mesh=mesh, in_specs=in_specs, out_specs=out_specs, check_vma=False
    )
```

```python
import functools
import itertools

import jax
import jax.numpy as jnp
import numpy as np
from jax import lax
from jax.experimental import pallas as pl
from jax.experimental.pallas import tpu as pltpu
from jax.sharding import PartitionSpec as P

MIB = 1024 * 1024
LOWEST = float(np.finfo(np.float32).min)
NO_PLAN = 2**30


def xor_permute(x, axis, k):
    size = lax.axis_size(axis)
    return lax.ppermute(x, axis, [(i, i ^ k) for i in range(size)])


def device_count():
    return lax.axis_size("dp") * lax.axis_size("vocab")


def exchange(copies):
    return lax.all_to_all(copies, ("dp", "vocab"), split_axis=0, concat_axis=0, tiled=True)


def log_sum_exp(values):
    top = jnp.max(values, axis=0, keepdims=True)
    return top + jnp.log(jnp.sum(jnp.exp(values - top), axis=0, keepdims=True))


def place(rows):
    return lambda k: pl.multiple_of((lax.axis_index("dp") ^ k) * rows, rows)


def student_kernel(n_chunks, *refs):
    chunk_refs = refs[:n_chunks]
    head_ref, teacher_ref, out_ref, hid_out_ref, stats_ref = refs[n_chunks : n_chunks + 5]
    hid_ref, rows_ref, logits_ref, scores_ref, top_ref, sum_ref, stat_ref = refs[n_chunks + 5 : -4]
    chunk_sems, head_sems, out_sems, sems = refs[-4:]
    tokens, rows = scores_ref.shape
    own = teacher_ref.shape[0]
    block = min(256, rows)
    blocks = rows // block

    def head_copy(i):
        here = pl.ds(pl.multiple_of(i * block, block), block)
        return pltpu.make_async_copy(head_ref.at[0, here], rows_ref.at[here], head_sems.at[i])

    def out_copy(i):
        here = pl.ds(pl.multiple_of(i * block, block), block)
        return pltpu.make_async_copy(scores_ref.at[:, here], out_ref.at[:, here], out_sems.at[i])

    teacher_copy = pltpu.make_async_copy(teacher_ref, logits_ref, sems.at[0])
    hid_copy = pltpu.make_async_copy(hid_ref, hid_out_ref, sems.at[1])
    copies = []
    for k, ref in enumerate(chunk_refs):
        copies.append(
            pltpu.make_async_copy(ref, hid_ref.at[k * own : (k + 1) * own], chunk_sems.at[k])
        )
    teacher_copy.start()
    for copy in copies:
        copy.start()
    for i in range(blocks):
        head_copy(i).start()

    top_ref[...] = jnp.full(top_ref.shape, LOWEST, jnp.float32)
    sum_ref[...] = jnp.zeros(sum_ref.shape, jnp.float32)
    teacher_copy.wait()
    values = logits_ref[...].astype(jnp.float32)
    top = jnp.max(values, axis=1, keepdims=True)
    total = jnp.sum(jnp.exp(values - top), axis=1, keepdims=True)
    stat = jnp.transpose(jnp.broadcast_to(top + jnp.log(total), (own, 128)))[0:1]
    stats_ref[:, :, tokens:] = jnp.broadcast_to(stat[None], (stats_ref.shape[0], 1, own))
    for copy in copies:
        copy.wait()
    hid_copy.start()

    def scores_of(i):
        columns = pl.ds(pl.multiple_of(i * block, block), block)
        scores_ref[:, columns] = lax.dot_general(
            hid_ref[...], rows_ref[columns], (((1,), (1,)), ((), ())), preferred_element_type=jnp.float32
        )

    def stats_of(i):
        values = scores_ref[:, pl.ds(pl.multiple_of(i * block, block), block)]
        old = top_ref[...]
        top = jnp.maximum(old, jnp.max(values, axis=1, keepdims=True))
        total = jnp.sum(jnp.exp(values - top), axis=1, keepdims=True)
        top_ref[...] = top
        sum_ref[...] = sum_ref[...] * jnp.exp(old - top) + total

    def step(i, carry):
        head_copy(i).wait()
        stats_of(i - 1)
        scores_of(i)
        out_copy(i - 1).start()
        return carry

    head_copy(0).wait()
    scores_of(0)
    lax.fori_loop(1, blocks, step, 0)
    out_copy(blocks - 1).start()
    stats_of(blocks - 1)
    at = place(own)
    for k in range(n_chunks):
        here = slice(k * own, (k + 1) * own)
        stat = top_ref[here] + jnp.log(sum_ref[here])
        stat_ref[pl.ds(at(k), own)] = jnp.broadcast_to(stat, (own, 128))
    stat = jnp.transpose(stat_ref[...])[0:1]
    stats_ref[:, :, :tokens] = jnp.broadcast_to(stat[None], (stats_ref.shape[0], 1, tokens))
    for i in range(blocks):
        out_copy(i).wait()
    hid_copy.wait()


def student_call(chunks, head, teacher, tokens):
    _, rows, depth = head.shape
    blocks = rows // min(256, rows)
    in_hbm = pl.BlockSpec(memory_space=pltpu.HBM)
    return pl.pallas_call(
        functools.partial(student_kernel, len(chunks)),
        in_specs=[in_hbm] * (len(chunks) + 2),
        out_specs=[in_hbm, in_hbm, pl.BlockSpec(memory_space=pltpu.VMEM)],
        out_shape=[
            jax.ShapeDtypeStruct((tokens, rows), jnp.float32),
            jax.ShapeDtypeStruct((tokens, depth), jnp.bfloat16),
            jax.ShapeDtypeStruct((device_count(), 1, tokens + teacher.shape[0]), jnp.float32),
        ],
        scratch_shapes=[
            pltpu.VMEM((tokens, depth), jnp.bfloat16),
            pltpu.VMEM((rows, depth), jnp.bfloat16),
            pltpu.VMEM(teacher.shape, jnp.bfloat16),
            pltpu.VMEM((tokens, rows), jnp.float32),
            pltpu.VMEM((tokens, 1), jnp.float32),
            pltpu.VMEM((tokens, 1), jnp.float32),
            pltpu.VMEM((tokens, 128), jnp.float32),
            pltpu.SemaphoreType.DMA((len(chunks),)),
            pltpu.SemaphoreType.DMA((blocks,)),
            pltpu.SemaphoreType.DMA((blocks,)),
            pltpu.SemaphoreType.DMA((2,)),
        ],
        compiler_params=pltpu.CompilerParams(vmem_limit_bytes=60 * MIB),
        cost_estimate=pl.CostEstimate(
            flops=2 * tokens * rows * depth,
            bytes_accessed=2 * rows * depth + 2 * tokens * depth + 4 * tokens * rows,
            transcendentals=tokens * rows,
        ),
        name="student",
    )(*chunks, head, teacher)


def cross_kernel(own_ref, got_ref, scores_ref, out_ref, col_ref):
    step, last = pl.program_id(0), pl.num_programs(0) - 1
    rows = scores_ref.shape[0]
    tokens = col_ref.shape[0]
    half = rows // 2
    at = place(rows)(step)
    core = lax.axis_index("vocab") & 1
    lane = lax.broadcasted_iota(jnp.int32, (half, 128), 1)
    for j, ref in enumerate((own_ref, got_ref)):
        first = pl.multiple_of((core ^ j) * half, half)
        target = ref[0].astype(jnp.float32)
        top = jnp.max(target, axis=1, keepdims=True)
        cross = jnp.exp(target - top) * (target - scores_ref[pl.ds(first, half)])
        col_ref[pl.ds(pl.multiple_of(at + first, half), half)] = jnp.where(
            lane == 0, top, jnp.sum(cross, axis=1, keepdims=True)
        )

    @pl.when(step == last)
    def _():
        lines = jnp.transpose(col_ref[...])
        for i in range(2):
            line = jnp.broadcast_to(lines[i : i + 1][None], (out_ref.shape[0], 1, tokens))
            out_ref[:, :, i * tokens : (i + 1) * tokens] = line


def cross_call(own, got, scores):
    n_dp, half, rows = own.shape
    tokens = 2 * n_dp * half
    shape = (device_count(), 1, 2 * tokens)
    return pl.pallas_call(
        cross_kernel,
        grid=(n_dp,),
        in_specs=[pl.BlockSpec((1, half, rows), lambda k: (k, 0, 0))] * 2
        + [pl.BlockSpec((2 * half, rows), lambda k: (k, 0))],
        out_specs=pl.BlockSpec(shape, lambda k: (0, 0, 0)),
        out_shape=jax.ShapeDtypeStruct(shape, jnp.float32),
        scratch_shapes=[pltpu.VMEM((tokens, 128), jnp.float32)],
        compiler_params=pltpu.CompilerParams(vmem_limit_bytes=24 * MIB),
        cost_estimate=pl.CostEstimate(
            flops=5 * tokens * rows, bytes_accessed=8 * tokens * rows, transcendentals=tokens * rows
        ),
        name="cross",
    )(own, got, scores)


def head_grad_kernel(
    own_ref, got_ref, scores_in_ref, hid_in_ref, stats_ref, weight_ref, out_ref, totals_ref,
    target_ref, scores_ref, hid_ref, grad_ref, col_ref, target_sems, scores_sems, hid_sem,
):
    n_dp, _, half, _ = target_ref.shape
    rows = 2 * half
    tokens = n_dp * rows
    block = out_ref.shape[1]
    step = pl.program_id(0)

    @pl.when(step == 0)
    def _():
        at, core = place(rows), lax.axis_index("vocab") & 1
        hid_copy = pltpu.make_async_copy(hid_in_ref, hid_ref, hid_sem)

        def target_copy(j, k):
            ref = (own_ref, got_ref)[j]
            return pltpu.make_async_copy(ref.at[k], target_ref.at[k, j], target_sems.at[2 * k + j])

        def scores_copy(k):
            here = pl.ds(pl.multiple_of(k * rows, rows), rows)
            return pltpu.make_async_copy(
                scores_in_ref.at[here], scores_ref.at[here], scores_sems.at[k]
            )

        for k in range(n_dp):
            scores_copy(k).start()
            target_copy(0, k).start()
            target_copy(1, k).start()
        hid_copy.start()
        n_vocab = stats_ref.shape[0] // n_dp
        total_s = log_sum_exp(stats_ref[:, 0, :tokens])
        total_t = jnp.concatenate(
            [
                log_sum_exp(stats_ref[d * n_vocab : (d + 1) * n_vocab, 0, tokens:])
                for d in range(n_dp)
            ],
            axis=1,
        )
        totals_ref[0:1] = total_s
        totals_ref[1:2] = total_t
        line = lax.broadcasted_iota(jnp.int32, (128, tokens), 0)
        col_ref[...] = jnp.transpose(
            jnp.where(line == 0, total_s, jnp.where(line == 1, total_t, weight_ref[...]))
        )

        def piece(k, carry):
            scores_copy(k).wait()
            for j in range(2):
                target_copy(j, k).wait()
                first = pl.multiple_of((core ^ j) * half, half)
                part = pl.ds(pl.multiple_of(k * rows + first, half), half)
                cols = col_ref[pl.ds(pl.multiple_of(at(k) + first, half), half)]
                target = target_ref[k, j].astype(jnp.float32)
                prob_s = jnp.exp(scores_ref[part] - cols[:, 0:1])
                prob_t = jnp.exp(target - cols[:, 1:2])
                grad_ref[part] = (cols[:, 2:3] * (prob_s - prob_t)).astype(jnp.bfloat16)
            return carry

        lax.fori_loop(0, n_dp, piece, 0)
        hid_copy.wait()

    ids = pl.ds(pl.multiple_of(step * block, block), block)
    out_ref[0] = lax.dot_general(
        grad_ref[:, ids], hid_ref[...], (((0,), (0,)), ((), ())), preferred_element_type=jnp.float32
    ).astype(jnp.bfloat16)


def head_grad_call(own, got, scores, hid, stats, weight):
    n_dp, half, rows = own.shape
    tokens, depth = hid.shape
    block = min(256, rows)
    in_hbm = pl.BlockSpec(memory_space=pltpu.HBM)
    return pl.pallas_call(
        head_grad_kernel,
        grid=(rows // block,),
        in_specs=[in_hbm] * 4
        + [pl.BlockSpec(stats.shape, lambda i: (0, 0, 0)), pl.BlockSpec((1, tokens), lambda i: (0, 0))],
        out_specs=[
            pl.BlockSpec((1, block, depth), lambda i: (0, i, 0)),
            pl.BlockSpec((2, tokens), lambda i: (0, 0)),
        ],
        out_shape=[
            jax.ShapeDtypeStruct((1, rows, depth), jnp.bfloat16),
            jax.ShapeDtypeStruct((2, tokens), jnp.float32),
        ],
        scratch_shapes=[
            pltpu.VMEM((n_dp, 2, half, rows), jnp.bfloat16),
            pltpu.VMEM((tokens, rows), jnp.float32),
            pltpu.VMEM((tokens, depth), jnp.bfloat16),
            pltpu.VMEM((tokens, rows), jnp.bfloat16),
            pltpu.VMEM((tokens, 128), jnp.float32),
            pltpu.SemaphoreType.DMA((2 * n_dp,)),
            pltpu.SemaphoreType.DMA((n_dp,)),
            pltpu.SemaphoreType.DMA,
        ],
        compiler_params=pltpu.CompilerParams(vmem_limit_bytes=60 * MIB),
        cost_estimate=pl.CostEstimate(
            flops=2 * tokens * rows * depth,
            bytes_accessed=2 * rows * depth + 2 * tokens * depth + 6 * tokens * rows,
            transcendentals=2 * tokens * rows,
        ),
        name="head_grad",
    )(own, got, scores, hid, stats, weight[None])


def chip_plans(n):
    def load(pair):
        ups = [sum(z < c <= p[z] for p in pair for z in range(n)) for c in range(1, n)]
        return max(ups), sum(ups)

    best = {}
    perms = list(itertools.permutations(range(n)))
    for pair in itertools.combinations_with_replacement(perms, 2):
        code = sum(3 ** (n * z + p[z]) for p in pair for z in range(n))
        if code not in best or load(pair) < load(best[code]):
            best[code] = pair
    return sorted(best.items())


def plan_tables(plans, n):
    codes = [code for code, _ in plans]
    keys = [
        (i << 8) | sum(first[z] << (2 * z) for z in range(n)) for i, (_, (first, _)) in enumerate(plans)
    ]
    pad = -len(codes) % 1024
    codes = np.array(codes + [-1] * pad, np.int32).reshape(-1, 128)
    keys = np.array(keys + [NO_PLAN] * pad, np.int32).reshape(-1, 128)
    return codes, keys


def plan_kernel(n_chips, order_ref, codes_ref, keys_ref, number_ref, flags_ref):
    me = lax.axis_index("vocab")
    chip, core = me // 2, me & 1
    code = jnp.int32(0)
    for block in range(2 * n_chips):
        dest = order_ref[block] // 2
        power = jnp.int32(0)
        for d in range(n_chips):
            power = jnp.where(dest == d, 3 ** (n_chips * (block // 2) + d), power)
        code = code + power
    key = jnp.min(jnp.where(codes_ref[...] == code, keys_ref[...], NO_PLAN))
    sends = jnp.int32(0)
    arrives = jnp.int32(0)
    for z in range(n_chips):
        goes = (key >> (2 * z)) & 3
        source = jnp.where(order_ref[2 * z] // 2 == goes, 0, 1)
        meant = jnp.where(source == 0, order_ref[2 * z], order_ref[2 * z + 1]) & 1
        sends = jnp.where(chip == z, source, sends)
        arrives = jnp.where(goes == chip, meant, arrives)
    number_ref[0] = key >> 8
    flags_ref[0] = (sends == core).astype(jnp.int32)
    flags_ref[1] = (arrives == core).astype(jnp.int32)


def plan_chips(shard_order, plans, n_chips):
    codes, keys = plan_tables(plans, n_chips)
    in_smem = pl.BlockSpec(memory_space=pltpu.SMEM)
    in_vmem = pl.BlockSpec(memory_space=pltpu.VMEM)
    return pl.pallas_call(
        functools.partial(plan_kernel, n_chips),
        in_specs=[in_smem, in_vmem, in_vmem],
        out_specs=[in_smem] * 2,
        out_shape=[jax.ShapeDtypeStruct((n,), jnp.int32) for n in (1, 2)],
        compiler_params=pltpu.CompilerParams(vmem_limit_bytes=60 * MIB),
        name="plan",
    )(shard_order, jnp.asarray(codes), jnp.asarray(keys))


def pick_kernel(flags_ref, mine_ref, other_ref, first_ref, second_ref):
    dp, core = lax.axis_index("dp"), lax.axis_index("vocab") & 1
    n_dp, half, cols = first_ref.shape
    rows = pl.ds(pl.multiple_of(core * half, half), half)
    own_first = flags_ref[0] != 0
    for k in range(n_dp):
        here = pl.ds(pl.multiple_of((dp ^ k) * cols, cols), cols)
        mine, other = mine_ref[rows, here], other_ref[rows, here]
        first_ref[k] = jnp.where(own_first, mine, other)
        second_ref[k] = jnp.where(own_first, other, mine)


def pick_call(flags, mine, other):
    n_dp = lax.axis_size("dp")
    shape = (n_dp, mine.shape[0] // 2, mine.shape[1] // n_dp)
    in_vmem = pl.BlockSpec(memory_space=pltpu.VMEM)
    return pl.pallas_call(
        pick_kernel,
        in_specs=[pl.BlockSpec(memory_space=pltpu.SMEM), in_vmem, in_vmem],
        out_specs=[in_vmem] * 2,
        out_shape=[jax.ShapeDtypeStruct(shape, jnp.bfloat16)] * 2,
        compiler_params=pltpu.CompilerParams(vmem_limit_bytes=24 * MIB),
        name="pick",
    )(flags, mine, other)


def pack_kernel(flags_ref, *refs):
    *piece_refs, own_ref, give_ref = refs
    own_first = flags_ref[1] != 0
    for k, ref in enumerate(piece_refs):
        first, second = ref[0], ref[1]
        own_ref[k] = jnp.where(own_first, first, second)
        give_ref[k] = jnp.where(own_first, second, first)


def pack_call(flags, pieces):
    in_vmem = pl.BlockSpec(memory_space=pltpu.VMEM)
    shape = (len(pieces), *pieces[0].shape[1:])
    return pl.pallas_call(
        pack_kernel,
        in_specs=[pl.BlockSpec(memory_space=pltpu.SMEM)] + [in_vmem] * len(pieces),
        out_specs=[in_vmem] * 2,
        out_shape=[jax.ShapeDtypeStruct(shape, jnp.bfloat16)] * 2,
        compiler_params=pltpu.CompilerParams(vmem_limit_bytes=24 * MIB),
        name="pack",
    )(flags, *pieces)


def halves(x):
    half = x.shape[0] // 2
    core = lax.axis_index("vocab") & 1
    mine = lax.dynamic_slice_in_dim(x, core * half, half, 0)
    return mine, lax.dynamic_slice_in_dim(x, (1 - core) * half, half, 0)


def over_dp(pieces):
    return [pieces[0]] + [xor_permute(pieces[k], "dp", k) for k in range(1, len(pieces))]


def wide_block(teacher, shard_order):
    token_rows = teacher.shape[0]
    n_vocab = lax.axis_size("vocab")
    piece_cols = teacher.shape[1] // n_vocab
    split_view = teacher.reshape(token_rows, n_vocab, piece_cols)
    spread_view = lax.all_to_all(split_view, "vocab", split_axis=1, concat_axis=1, tiled=True)
    ordinal = jnp.arange(n_vocab, dtype=jnp.int32)
    matches = (shard_order[None, :] == ordinal[:, None]).astype(jnp.int32)
    inverse = jnp.sum(matches * ordinal[None, :], axis=1)
    sorted_view = jnp.take(spread_view, inverse, axis=1)
    return lax.all_to_all(sorted_view, "vocab", split_axis=1, concat_axis=1, tiled=True).reshape(
        token_rows, n_vocab * piece_cols
    )


def on_device(hidden, head, teacher, shard_order, loss_weight):
    n_dp, n_vocab = lax.axis_size("dp"), lax.axis_size("vocab")
    n_chips = n_vocab // 2
    tokens = hidden.shape[0] * n_dp

    if n_chips <= 4:
        other = xor_permute(teacher, "vocab", 1)
        plans = chip_plans(n_chips)
        number, flags = plan_chips(shard_order, plans, n_chips)
        chunks = [hidden] + [xor_permute(hidden, "dp", k) for k in range(1, n_dp)]

        def over_chips(x, perm):
            if perm == tuple(range(n_chips)):
                return x
            pairs = [(2 * z + c, 2 * perm[z] + c) for z in range(n_chips) for c in range(2)]
            return lax.ppermute(x, "vocab", pairs)

        def follow(x, y, pair):
            return over_chips(x, pair[0]), over_chips(y, pair[1])

        arrived = lax.switch(
            number[0],
            [functools.partial(follow, pair=pair) for _, pair in plans],
            *pick_call(flags, teacher, other),
        )
        chunks, arrived = lax.optimization_barrier((chunks, arrived))
        pieces = over_dp([jnp.stack([x[k] for x in arrived]) for k in range(n_dp)])
        student, hid, stats = student_call(chunks, head, teacher, tokens)
        pieces, _ = lax.optimization_barrier((pieces, stats))
        own, give = pack_call(flags, pieces)
        got = xor_permute(give, "vocab", 1)
    else:
        chunks = [hidden] + [xor_permute(hidden, "dp", k) for k in range(1, n_dp)]
        student, hid, stats = student_call(chunks, head, teacher, tokens)
        block = wide_block(teacher, shard_order)
        cols, dp = block.shape[1] // n_dp, lax.axis_index("dp")
        pieces = over_dp(
            [lax.dynamic_slice_in_dim(block, (dp ^ k) * cols, cols, 1) for k in range(n_dp)]
        )
        own, got = (jnp.stack(x) for x in zip(*(halves(piece) for piece in pieces)))

    sent = cross_call(own, got, student)
    parts, sent = lax.optimization_barrier((exchange(stats), sent))
    head_grad, totals = head_grad_call(own, got, student, hid, parts, loss_weight)
    parts, head_grad = lax.optimization_barrier((exchange(sent), head_grad))
    total_s, total_t = totals[0], totals[1]
    tops, terms = parts[:, 0, :tokens], parts[:, 0, tokens:]
    divergence = jnp.sum(terms * jnp.exp(tops - total_t), axis=0) - total_t + total_s
    return head_grad, divergence


def solution(mesh):
    in_specs = (P("dp", None), P("dp", "vocab", None), P("dp", "vocab"), P(), P())
    out_specs = (P("dp", "vocab", None), P())
    return jax.shard_map(
        on_device, mesh=mesh, in_specs=in_specs, out_specs=out_specs, check_vma=False
    )
```

```python
import functools
import itertools

import jax
import jax.numpy as jnp
import numpy as np
from jax import lax
from jax.experimental import pallas as pl
from jax.experimental.pallas import tpu as pltpu
from jax.sharding import PartitionSpec as P

MIB = 1024 * 1024
LOWEST = float(np.finfo(np.float32).min)
NO_PLAN = 2**30


def xor_permute(x, axis, k):
    size = lax.axis_size(axis)
    return lax.ppermute(x, axis, [(i, i ^ k) for i in range(size)])


def device_count():
    return lax.axis_size("dp") * lax.axis_size("vocab")


def exchange(copies):
    return lax.all_to_all(copies, ("dp", "vocab"), split_axis=0, concat_axis=0, tiled=True)


def log_sum_exp(values):
    top = jnp.max(values, axis=0, keepdims=True)
    return top + jnp.log(jnp.sum(jnp.exp(values - top), axis=0, keepdims=True))


def place(rows):
    return lambda k: pl.multiple_of((lax.axis_index("dp") ^ k) * rows, rows)


def student_kernel(n_chunks, *refs):
    chunk_refs = refs[:n_chunks]
    head_ref, teacher_ref, out_ref, hid_out_ref, stats_ref = refs[n_chunks : n_chunks + 5]
    hid_ref, rows_ref, logits_ref, scores_ref, top_ref, sum_ref, stat_ref = refs[n_chunks + 5 : -4]
    chunk_sems, head_sems, out_sems, sems = refs[-4:]
    tokens, rows = scores_ref.shape
    own = teacher_ref.shape[0]
    block = min(256, rows)
    blocks = rows // block

    def head_copy(i):
        here = pl.ds(pl.multiple_of(i * block, block), block)
        return pltpu.make_async_copy(head_ref.at[0, here], rows_ref.at[here], head_sems.at[i])

    def out_copy(i):
        here = pl.ds(pl.multiple_of(i * block, block), block)
        return pltpu.make_async_copy(scores_ref.at[:, here], out_ref.at[:, here], out_sems.at[i])

    teacher_copy = pltpu.make_async_copy(teacher_ref, logits_ref, sems.at[0])
    hid_copy = pltpu.make_async_copy(hid_ref, hid_out_ref, sems.at[1])
    copies = []
    for k, ref in enumerate(chunk_refs):
        copies.append(
            pltpu.make_async_copy(ref, hid_ref.at[k * own : (k + 1) * own], chunk_sems.at[k])
        )
    teacher_copy.start()
    for copy in copies:
        copy.start()
    for i in range(blocks):
        head_copy(i).start()

    top_ref[...] = jnp.full(top_ref.shape, LOWEST, jnp.float32)
    sum_ref[...] = jnp.zeros(sum_ref.shape, jnp.float32)
    teacher_copy.wait()
    values = logits_ref[...].astype(jnp.float32)
    top = jnp.max(values, axis=1, keepdims=True)
    total = jnp.sum(jnp.exp(values - top), axis=1, keepdims=True)
    stat = jnp.transpose(jnp.broadcast_to(top + jnp.log(total), (own, 128)))[0:1]
    stats_ref[:, :, tokens:] = jnp.broadcast_to(stat[None], (stats_ref.shape[0], 1, own))
    for copy in copies:
        copy.wait()
    hid_copy.start()

    def scores_of(i):
        columns = pl.ds(pl.multiple_of(i * block, block), block)
        scores_ref[:, columns] = lax.dot_general(
            hid_ref[...], rows_ref[columns], (((1,), (1,)), ((), ())), preferred_element_type=jnp.float32
        )

    def stats_of(i):
        values = scores_ref[:, pl.ds(pl.multiple_of(i * block, block), block)]
        old = top_ref[...]
        top = jnp.maximum(old, jnp.max(values, axis=1, keepdims=True))
        total = jnp.sum(jnp.exp(values - top), axis=1, keepdims=True)
        top_ref[...] = top
        sum_ref[...] = sum_ref[...] * jnp.exp(old - top) + total

    def step(i, carry):
        head_copy(i).wait()
        stats_of(i - 1)
        scores_of(i)
        out_copy(i - 1).start()
        return carry

    head_copy(0).wait()
    scores_of(0)
    lax.fori_loop(1, blocks, step, 0)
    out_copy(blocks - 1).start()
    stats_of(blocks - 1)
    at = place(own)
    for k in range(n_chunks):
        here = slice(k * own, (k + 1) * own)
        stat = top_ref[here] + jnp.log(sum_ref[here])
        stat_ref[pl.ds(at(k), own)] = jnp.broadcast_to(stat, (own, 128))
    stat = jnp.transpose(stat_ref[...])[0:1]
    stats_ref[:, :, :tokens] = jnp.broadcast_to(stat[None], (stats_ref.shape[0], 1, tokens))
    for i in range(blocks):
        out_copy(i).wait()
    hid_copy.wait()


def student_call(chunks, head, teacher, tokens):
    _, rows, depth = head.shape
    blocks = rows // min(256, rows)
    in_hbm = pl.BlockSpec(memory_space=pltpu.HBM)
    return pl.pallas_call(
        functools.partial(student_kernel, len(chunks)),
        in_specs=[in_hbm] * (len(chunks) + 2),
        out_specs=[in_hbm, in_hbm, pl.BlockSpec(memory_space=pltpu.VMEM)],
        out_shape=[
            jax.ShapeDtypeStruct((tokens, rows), jnp.float32),
            jax.ShapeDtypeStruct((tokens, depth), jnp.bfloat16),
            jax.ShapeDtypeStruct((device_count(), 1, tokens + teacher.shape[0]), jnp.float32),
        ],
        scratch_shapes=[
            pltpu.VMEM((tokens, depth), jnp.bfloat16),
            pltpu.VMEM((rows, depth), jnp.bfloat16),
            pltpu.VMEM(teacher.shape, jnp.bfloat16),
            pltpu.VMEM((tokens, rows), jnp.float32),
            pltpu.VMEM((tokens, 1), jnp.float32),
            pltpu.VMEM((tokens, 1), jnp.float32),
            pltpu.VMEM((tokens, 128), jnp.float32),
            pltpu.SemaphoreType.DMA((len(chunks),)),
            pltpu.SemaphoreType.DMA((blocks,)),
            pltpu.SemaphoreType.DMA((blocks,)),
            pltpu.SemaphoreType.DMA((2,)),
        ],
        compiler_params=pltpu.CompilerParams(vmem_limit_bytes=60 * MIB),
        cost_estimate=pl.CostEstimate(
            flops=2 * tokens * rows * depth,
            bytes_accessed=2 * rows * depth + 2 * tokens * depth + 4 * tokens * rows,
            transcendentals=tokens * rows,
        ),
        name="student",
    )(*chunks, head, teacher)


def cross_kernel(flags_ref, mine_ref, got_ref, scores_ref, out_ref, col_ref):
    step, last = pl.program_id(0), pl.num_programs(0) - 1
    rows = scores_ref.shape[0]
    tokens = col_ref.shape[0]
    half = rows // 2
    at = place(rows)(step)
    keep = flags_ref[1] != 0
    lane = lax.broadcasted_iota(jnp.int32, (half, 128), 1)
    for first in (0, half):
        part = slice(first, first + half)
        here = pl.ds(pl.multiple_of(at + first, half), half)
        target = jnp.where(keep, mine_ref[0, part], got_ref[0, part]).astype(jnp.float32)
        top = jnp.max(target, axis=1, keepdims=True)
        cross = jnp.exp(target - top) * (target - scores_ref[part])
        col_ref[here] = jnp.where(lane == 0, top, jnp.sum(cross, axis=1, keepdims=True))

    @pl.when(step == last)
    def _():
        lines = jnp.transpose(col_ref[...])
        for i in range(2):
            line = jnp.broadcast_to(lines[i : i + 1][None], (out_ref.shape[0], 1, tokens))
            out_ref[:, :, i * tokens : (i + 1) * tokens] = line


def block_specs(n_dp, part, rows):
    return [
        pl.BlockSpec(memory_space=pltpu.SMEM),
        pl.BlockSpec((1, part, rows), lambda k: (k, 0, 0)),
        pl.BlockSpec((1, part, rows), lambda k: (k, 0, 0)),
        pl.BlockSpec((part, rows), lambda k: (k, 0)),
    ]


def cross_call(flags, mine, got, scores):
    n_dp, part, rows = mine.shape
    tokens = n_dp * part
    shape = (device_count(), 1, 2 * tokens)
    return pl.pallas_call(
        cross_kernel,
        grid=(n_dp,),
        in_specs=block_specs(n_dp, part, rows),
        out_specs=pl.BlockSpec(shape, lambda k: (0, 0, 0)),
        out_shape=jax.ShapeDtypeStruct(shape, jnp.float32),
        scratch_shapes=[pltpu.VMEM((tokens, 128), jnp.float32)],
        compiler_params=pltpu.CompilerParams(vmem_limit_bytes=24 * MIB),
        cost_estimate=pl.CostEstimate(
            flops=5 * tokens * rows, bytes_accessed=8 * tokens * rows, transcendentals=tokens * rows
        ),
        name="cross",
    )(flags, mine, got, scores)


def head_grad_kernel(
    flags_ref, mine_ref, got_ref, scores_in_ref, hid_in_ref, stats_ref, weight_ref, out_ref,
    total_s_ref, total_t_ref, target_ref, scores_ref, hid_ref, grad_ref, col_ref, target_sems, scores_sems, hid_sem,
):
    n_dp, rows, _ = target_ref.shape
    tokens = n_dp * rows
    block = out_ref.shape[1]
    step = pl.program_id(0)

    @pl.when(step == 0)
    def _():
        at = place(rows)
        half = rows // 2
        hid_copy = pltpu.make_async_copy(hid_in_ref, hid_ref, hid_sem)

        def target_copy(ref, k):
            return pltpu.make_async_copy(ref.at[k], target_ref.at[k], target_sems.at[k])

        def scores_copy(k):
            here = pl.ds(pl.multiple_of(k * rows, rows), rows)
            return pltpu.make_async_copy(
                scores_in_ref.at[here], scores_ref.at[here], scores_sems.at[k]
            )

        for k in range(n_dp):
            scores_copy(k).start()

            @pl.when(flags_ref[1] != 0)
            def _():
                target_copy(mine_ref, k).start()

            @pl.when(flags_ref[1] == 0)
            def _():
                target_copy(got_ref, k).start()

        hid_copy.start()
        n_vocab = stats_ref.shape[0] // n_dp
        total_s = log_sum_exp(stats_ref[:, 0, :tokens])
        total_t = jnp.concatenate(
            [
                log_sum_exp(stats_ref[d * n_vocab : (d + 1) * n_vocab, 0, tokens:])
                for d in range(n_dp)
            ],
            axis=1,
        )
        total_s_ref[...] = total_s
        total_t_ref[...] = total_t
        line = lax.broadcasted_iota(jnp.int32, (128, tokens), 0)
        col_ref[...] = jnp.transpose(
            jnp.where(line == 0, total_s, jnp.where(line == 1, total_t, weight_ref[...]))
        )

        def piece(k, carry):
            scores_copy(k).wait()
            target_copy(mine_ref, k).wait()
            for first in (0, half):
                part = pl.ds(pl.multiple_of(k * rows + first, half), half)
                cols = col_ref[pl.ds(pl.multiple_of(at(k) + first, half), half)]
                target = target_ref[k, first : first + half].astype(jnp.float32)
                prob_s = jnp.exp(scores_ref[part] - cols[:, 0:1])
                prob_t = jnp.exp(target - cols[:, 1:2])
                grad_ref[part] = (cols[:, 2:3] * (prob_s - prob_t)).astype(jnp.bfloat16)
            return carry

        lax.fori_loop(0, n_dp, piece, 0)
        hid_copy.wait()

    ids = pl.ds(pl.multiple_of(step * block, block), block)
    out_ref[0] = lax.dot_general(
        grad_ref[:, ids], hid_ref[...], (((0,), (0,)), ((), ())), preferred_element_type=jnp.float32
    ).astype(jnp.bfloat16)


def head_grad_call(flags, mine, got, scores, hid, stats, weight):
    n_dp, part, rows = mine.shape
    tokens, depth = hid.shape
    block = min(256, rows)
    in_hbm = pl.BlockSpec(memory_space=pltpu.HBM)
    return pl.pallas_call(
        head_grad_kernel,
        grid=(rows // block,),
        in_specs=[pl.BlockSpec(memory_space=pltpu.SMEM)] + [in_hbm] * 4
        + [pl.BlockSpec(stats.shape, lambda i: (0, 0, 0)), pl.BlockSpec((1, tokens), lambda i: (0, 0))],
        out_specs=[
            pl.BlockSpec((1, block, depth), lambda i: (0, i, 0)),
            pl.BlockSpec((1, tokens), lambda i: (0, 0)),
            pl.BlockSpec((1, tokens), lambda i: (0, 0)),
        ],
        out_shape=[
            jax.ShapeDtypeStruct((1, rows, depth), jnp.bfloat16),
            jax.ShapeDtypeStruct((1, tokens), jnp.float32),
            jax.ShapeDtypeStruct((1, tokens), jnp.float32),
        ],
        scratch_shapes=[
            pltpu.VMEM(mine.shape, jnp.bfloat16),
            pltpu.VMEM((tokens, rows), jnp.float32),
            pltpu.VMEM((tokens, depth), jnp.bfloat16),
            pltpu.VMEM((tokens, rows), jnp.bfloat16),
            pltpu.VMEM((tokens, 128), jnp.float32),
            pltpu.SemaphoreType.DMA((n_dp,)),
            pltpu.SemaphoreType.DMA((n_dp,)),
            pltpu.SemaphoreType.DMA,
        ],
        compiler_params=pltpu.CompilerParams(vmem_limit_bytes=60 * MIB),
        cost_estimate=pl.CostEstimate(
            flops=2 * tokens * rows * depth,
            bytes_accessed=2 * rows * depth + 2 * tokens * depth + 6 * tokens * rows,
            transcendentals=2 * tokens * rows,
        ),
        name="head_grad",
    )(flags, mine, got, scores, hid, stats, weight[None])


def chip_plans(n):
    def load(pair):
        ups = [sum(z < c <= p[z] for p in pair for z in range(n)) for c in range(1, n)]
        return max(ups), sum(ups)

    best = {}
    perms = list(itertools.permutations(range(n)))
    for pair in itertools.combinations_with_replacement(perms, 2):
        code = sum(3 ** (n * z + p[z]) for p in pair for z in range(n))
        if code not in best or load(pair) < load(best[code]):
            best[code] = pair
    return sorted(best.items())


def plan_tables(plans, n):
    codes = [code for code, _ in plans]
    keys = [
        (i << 8) | sum(first[z] << (2 * z) for z in range(n)) for i, (_, (first, _)) in enumerate(plans)
    ]
    pad = -len(codes) % 1024
    codes = np.array(codes + [-1] * pad, np.int32).reshape(-1, 128)
    keys = np.array(keys + [NO_PLAN] * pad, np.int32).reshape(-1, 128)
    return codes, keys


def plan_kernel(n_chips, order_ref, codes_ref, keys_ref, number_ref, flags_ref):
    chip = lax.axis_index("vocab") // 2
    code = jnp.int32(0)
    for block in range(2 * n_chips):
        dest = order_ref[block] // 2
        power = jnp.int32(0)
        for d in range(n_chips):
            power = jnp.where(dest == d, 3 ** (n_chips * (block // 2) + d), power)
        code = code + power
    key = jnp.min(jnp.where(codes_ref[...] == code, keys_ref[...], NO_PLAN))
    sends = jnp.int32(0)
    arrives = jnp.int32(0)
    for z in range(n_chips):
        goes = (key >> (2 * z)) & 3
        source = jnp.where(order_ref[2 * z] // 2 == goes, 0, 1)
        meant = jnp.where(source == 0, order_ref[2 * z], order_ref[2 * z + 1]) & 1
        sends = jnp.where(chip == z, source, sends)
        arrives = jnp.where(goes == chip, meant, arrives)
    number_ref[0] = key >> 8
    flags_ref[0] = 1 - sends
    flags_ref[1] = 1 - arrives


def plan_chips(shard_order, plans, n_chips):
    codes, keys = plan_tables(plans, n_chips)
    in_smem = pl.BlockSpec(memory_space=pltpu.SMEM)
    in_vmem = pl.BlockSpec(memory_space=pltpu.VMEM)
    return pl.pallas_call(
        functools.partial(plan_kernel, n_chips),
        in_specs=[in_smem, in_vmem, in_vmem],
        out_specs=[in_smem] * 2,
        out_shape=[jax.ShapeDtypeStruct((n,), jnp.int32) for n in (1, 2)],
        compiler_params=pltpu.CompilerParams(vmem_limit_bytes=60 * MIB),
        name="plan",
    )(shard_order, jnp.asarray(codes), jnp.asarray(keys))


def pick_kernel(flags_ref, mine_ref, other_ref, out_ref):
    dp = lax.axis_index("dp")
    n_dp, _, cols = out_ref.shape
    own = flags_ref[0] != 0
    for k in range(n_dp):
        here = pl.ds(pl.multiple_of((dp ^ k) * cols, cols), cols)
        out_ref[k] = jnp.where(own, mine_ref[:, here], other_ref[:, here])


def pick_call(flags, mine, other):
    n_dp = lax.axis_size("dp")
    shape = (n_dp, mine.shape[0], mine.shape[1] // n_dp)
    in_vmem = pl.BlockSpec(memory_space=pltpu.VMEM)
    return pl.pallas_call(
        pick_kernel,
        in_specs=[pl.BlockSpec(memory_space=pltpu.SMEM), in_vmem, in_vmem],
        out_specs=in_vmem,
        out_shape=jax.ShapeDtypeStruct(shape, jnp.bfloat16),
        compiler_params=pltpu.CompilerParams(vmem_limit_bytes=24 * MIB),
        name="pick",
    )(flags, mine, other)


def join_kernel(*refs):
    for k, ref in enumerate(refs[:-1]):
        refs[-1][k] = ref[...]


def join_call(pieces):
    in_vmem = pl.BlockSpec(memory_space=pltpu.VMEM)
    return pl.pallas_call(
        join_kernel,
        in_specs=[in_vmem] * len(pieces),
        out_specs=in_vmem,
        out_shape=jax.ShapeDtypeStruct((len(pieces), *pieces[0].shape), jnp.bfloat16),
        compiler_params=pltpu.CompilerParams(vmem_limit_bytes=24 * MIB),
        name="join",
    )(*pieces)


def over_dp(pieces):
    return [pieces[0]] + [xor_permute(pieces[k], "dp", k) for k in range(1, len(pieces))]


def wide_block(teacher, shard_order):
    token_rows = teacher.shape[0]
    n_vocab = lax.axis_size("vocab")
    piece_cols = teacher.shape[1] // n_vocab
    split_view = teacher.reshape(token_rows, n_vocab, piece_cols)
    spread_view = lax.all_to_all(split_view, "vocab", split_axis=1, concat_axis=1, tiled=True)
    ordinal = jnp.arange(n_vocab, dtype=jnp.int32)
    matches = (shard_order[None, :] == ordinal[:, None]).astype(jnp.int32)
    inverse = jnp.sum(matches * ordinal[None, :], axis=1)
    sorted_view = jnp.take(spread_view, inverse, axis=1)
    return lax.all_to_all(sorted_view, "vocab", split_axis=1, concat_axis=1, tiled=True).reshape(
        token_rows, n_vocab * piece_cols
    )


def on_device(hidden, head, teacher, shard_order, loss_weight):
    n_dp, n_vocab = lax.axis_size("dp"), lax.axis_size("vocab")
    n_chips = n_vocab // 2
    tokens = hidden.shape[0] * n_dp

    if n_chips <= 4:
        other = xor_permute(teacher, "vocab", 1)
        plans = chip_plans(n_chips)
        number, flags = plan_chips(shard_order, plans, n_chips)
        chunks = [hidden] + [xor_permute(hidden, "dp", k) for k in range(1, n_dp)]

        def over_chips(x, pair):
            pairs = [(2 * z + c, 2 * pair[c][z] + c) for z in range(n_chips) for c in range(2)]
            return lax.ppermute(x, "vocab", pairs)

        arrived = lax.switch(
            number[0],
            [functools.partial(over_chips, pair=pair) for _, pair in plans],
            pick_call(flags, teacher, other),
        )
        chunks, arrived = lax.optimization_barrier((chunks, arrived))
        pieces = over_dp([arrived[k] for k in range(n_dp)])
        student, hid, stats = student_call(chunks, head, teacher, tokens)
        pieces, _ = lax.optimization_barrier((pieces, stats))
        mine = join_call(pieces)
        got = xor_permute(mine, "vocab", 1)
    else:
        chunks = [hidden] + [xor_permute(hidden, "dp", k) for k in range(1, n_dp)]
        student, hid, stats = student_call(chunks, head, teacher, tokens)
        block = wide_block(teacher, shard_order)
        cols, dp = block.shape[1] // n_dp, lax.axis_index("dp")
        mine = jnp.stack(
            over_dp([lax.dynamic_slice_in_dim(block, (dp ^ k) * cols, cols, 1) for k in range(n_dp)])
        )
        flags, got = jnp.ones((2,), jnp.int32), mine

    sent = cross_call(flags, mine, got, student)
    parts, sent = lax.optimization_barrier((exchange(stats), sent))
    head_grad, total_s, total_t = head_grad_call(flags, mine, got, student, hid, parts, loss_weight)
    parts, head_grad = lax.optimization_barrier((exchange(sent), head_grad))
    total_s, total_t = total_s[0], total_t[0]
    tops, terms = parts[:, 0, :tokens], parts[:, 0, tokens:]
    divergence = jnp.sum(terms * jnp.exp(tops - total_t), axis=0) - total_t + total_s
    return head_grad, divergence


def solution(mesh):
    in_specs = (P("dp", None), P("dp", "vocab", None), P("dp", "vocab"), P(), P())
    out_specs = (P("dp", "vocab", None), P())
    return jax.shard_map(
        on_device, mesh=mesh, in_specs=in_specs, out_specs=out_specs, check_vma=False
    )
```
